128 devices in a mesh: replica: 4 (over x_hi, core), fsdp: 32 (over y, z, x_lo).
Axes of the slice: x: 4 (x_hi: 2, x_lo: 2; x = x_hi * 2 + x_lo), y: 4, z: 4, core: 2. Of those that a mesh axis runs over, the one named last changes fastest.
Arguments:
- tokens: bfloat16 [98304, 8192], P(('replica', 'fsdp')), may hold values from -24 to 24
- sign_bits: int32 [8192], replicated, may hold values from 0 to 1
- base_weight: bfloat16 [8192, 1024], P('fsdp'), may hold values from -0.0625 to 0.0625
- learned_column_scale: float32 [1024], replicated, may hold values from 0.5 to 2
- adapter_in: bfloat16 [4, 8192, 256], P('replica', 'fsdp'), may hold values from -0.0625 to 0.0625
- adapter_up_weight: bfloat16 [4, 256, 1024], P('replica'), may hold values from -0.375 to 0.375
- out_cotangent: bfloat16 [98304, 1024], P(('replica', 'fsdp')), may hold values from -6 to 6
- local_left: float32 [4, 4, 8192, 256], P('replica', None, 'fsdp'), may hold values from -6 to 6
- local_right: float32 [4, 4, 256, 1024], P('replica', None, 'fsdp'), may hold values from -6 to 6
- global_left: float32 [4, 8192, 256], P(None, 'fsdp'), may hold values from -6 to 6
- global_right: float32 [4, 256, 1024], P(None, 'fsdp'), may hold values from -6 to 6
- moment_left: float32 [4, 8192, 256], P(None, 'fsdp'), may hold values from -4 to 4
- moment_right: float32 [4, 256, 1024], P(None, 'fsdp'), may hold values from -4 to 4
- pending_left: float32 [4, 8192, 256], P(None, 'fsdp'), may hold values from -6 to 6
- pending_right: float32 [4, 256, 1024], P(None, 'fsdp'), may hold values from -6 to 6
Outputs:
- values: bfloat16 [98304, 1024], P(('replica', 'fsdp'))
- grad_in: float32 [4, 8192, 256], P('replica', 'fsdp')
- grad_out: float32 [4, 256, 1024], P('replica', 'fsdp')
- grad_scale: float32 [4, 1024], P('replica')
- next_global_left: float32 [4, 8192, 256], P(None, 'fsdp')
- next_global_right: float32 [4, 256, 1024], P(None, 'fsdp')
- next_moment_left: float32 [4, 8192, 256], P(None, 'fsdp')
- next_moment_right: float32 [4, 256, 1024], P(None, 'fsdp')
- next_pending_left: float32 [4, 8192, 256], P(None, 'fsdp')
- next_pending_right: float32 [4, 256, 1024], P(None, 'fsdp')
The draws below stay inside these ranges and needn't reach their ends.
All inputs are finite; a program needn't handle non-finite values.
Results may differ from the reference program's by a relative error of at most 0.012.
Values may be sent and summed in bfloat16 or wider, within the bound.
A program may use at most 192 MiB of HBM per device.

```python
import math
import jax
import jax.numpy as jnp
from jax import lax

D = 8192
V = 1024
R = 256
FRAG = 4
REP_TOKENS = 24576
TOKENS = 98304
N_REPLICA = 4


def plant(array, stream_key, low, high):
    index_at = [jax.random.randint(jax.random.fold_in(stream_key, axis), (), 0, length) for axis, length in enumerate(array.shape)]
    widest = array.shape.index(max(array.shape))
    next_to = index_at[:widest] + [(index_at[widest] + 1) % array.shape[widest]] + index_at[widest + 1:]
    return array.at[tuple(index_at)].set(low).at[tuple(next_to)].set(high)


def raised(result, rng, source, target, blocks, factor):
    def block_of(position):
        return (jnp.arange(result.shape[position]) // (result.shape[position] // blocks)).reshape((-1,) + (1,) * (result.ndim - 1 - position))

    one_side = jax.random.permutation(rng, blocks)[block_of(target)]
    far = (block_of(target) + blocks // 2) % blocks
    return jnp.where((block_of(source) == one_side) | (block_of(source) == far), factor * result, result)


def shard_levels(key, shape, shards, smallest, top_value):
    gain, own = 1.0, jax.random.fold_in(key, 6)
    for axis_at, parts in shards:
        heights = jnp.exp(jax.random.uniform(jax.random.fold_in(own, axis_at), (parts,), jnp.float32, smallest / len(shards), top_value / len(shards)))
        gain = gain * jnp.repeat(heights, shape[axis_at] // parts).reshape([-1 if axis == axis_at else 1 for axis in range(len(shape))])
    return gain


def normal_values(own_key, extent, scale, limit, shards=(), kind=jnp.bfloat16):
    drawn = scale * jax.random.normal(own_key, extent, jnp.float32)
    if shards:
        drawn = drawn * shard_levels(own_key, extent, shards, -0.22, 0.18)
    return jnp.clip(drawn, -limit, limit).astype(kind)


def bell_draw_with(own_key, extent, width, limit, cuts, heavy, held_as=jnp.bfloat16):
    array = width * jax.random.normal(own_key, extent, jnp.float32)
    if cuts:
        array = array * shard_levels(own_key, extent, cuts, -0.22, 0.18)
    return jnp.clip(raised(array, jax.random.fold_in(own_key, 3), *heavy), -limit, limit).astype(held_as)


def setup_inputs(seed: int = 0) -> dict:
    seeds = jax.random.split(jax.random.key(seed), 16)
    return {
        "tokens": bell_draw_with(seeds[0], (TOKENS, D), 1.0, 24.0, ((0, 128),), (0, 1, 128, 5.5)),
        "sign_bits": plant(jax.random.randint(seeds[1], (D,), 0, 2), jax.random.fold_in(seeds[1], 1), 0, 1).astype(jnp.int32),
        "base_weight": normal_values(seeds[2], (D, V), D ** -0.5, 0.0625, ((0, 32),)),
        "learned_column_scale": jnp.clip(jnp.exp(jax.random.uniform(seeds[3], (V,), jnp.float32, math.log(0.5), math.log(2.0))), 0.5, 2.0),
        "adapter_in": normal_values(seeds[4], (N_REPLICA, D, R), D ** -0.5, 0.0625, ((0, 4), (1, 32))),
        "adapter_up_weight": normal_values(seeds[5], (N_REPLICA, R, V), R ** -0.5, 0.375, ((0, 4),)),
        "out_cotangent": normal_values(seeds[6], (TOKENS, V), 1.0, 6.0, ((0, 128),)),
        "local_left": normal_values(seeds[7], (N_REPLICA, FRAG, D, R), 1.0, 6.0, ((0, 4), (2, 32)), jnp.float32),
        "local_right": normal_values(seeds[8], (N_REPLICA, FRAG, R, V), 1.0, 6.0, ((0, 4), (2, 32)), jnp.float32),
        "global_left": normal_values(seeds[9], (FRAG, D, R), 1.0, 6.0, ((1, 32),), jnp.float32),
        "global_right": normal_values(seeds[10], (FRAG, R, V), 1.0, 6.0, ((1, 32),), jnp.float32),
        "moment_left": normal_values(seeds[11], (FRAG, D, R), 0.5, 4.0, ((1, 32),), jnp.float32),
        "moment_right": normal_values(seeds[12], (FRAG, R, V), 0.5, 4.0, ((1, 32),), jnp.float32),
        "pending_left": normal_values(seeds[13], (FRAG, D, R), 1.0, 6.0, ((1, 32),), jnp.float32),
        "pending_right": normal_values(seeds[14], (FRAG, R, V), 1.0, 6.0, ((1, 32),), jnp.float32),
    }


ADAPTER_SCALE = 2.0
MOMENTUM = 0.9
OUTER_RATE = 0.7

def hadamard_matrix(order_size):
    indices = jnp.arange(order_size, dtype=jnp.int32)
    parity = jnp.zeros((order_size, order_size), jnp.int32)
    for bit_pos in range(order_size.bit_length() - 1):
        upper = jnp.bitwise_and(jnp.right_shift(indices, bit_pos), 1)
        parity = parity + upper[:, None] * upper[None, :]
    return (1 - 2 * (parity % 2)).astype(jnp.float32)

def rotate(tokens, sign_bits):
    features = tokens.shape[1]
    block_list = features // 128
    sign_flipped = tokens * (1 - 2 * sign_bits).astype(jnp.bfloat16)
    first_section = jnp.einsum('lvr,rq->lvq', sign_flipped.reshape(-1, block_list, 128).astype(jnp.float32), hadamard_matrix(128)).astype(jnp.bfloat16)
    section_two = jnp.einsum('tab,ac->tcb', first_section.astype(jnp.float32), hadamard_matrix(block_list)) * (1.0 / math.sqrt(features))
    return section_two.astype(jnp.bfloat16).reshape(-1, features)

def reference(tokens, sign_bits, base_weight, learned_column_scale, adapter_in, adapter_up_weight, out_cotangent, local_left, local_right, global_left, global_right, moment_left, moment_right, pending_left, pending_right):
    shrink_factor = 1.0 / math.sqrt(REP_TOKENS)
    value_list, in_list, output_list, scale_list = ([], [], [], [])
    for replica_index in range(N_REPLICA):
        rows = tokens[replica_index * REP_TOKENS:(replica_index + 1) * REP_TOKENS]
        output_gradient = out_cotangent[replica_index * REP_TOKENS:(replica_index + 1) * REP_TOKENS]
        rotated = rotate(rows, sign_bits)
        frozen_output = jnp.dot(rotated, base_weight, preferred_element_type=jnp.float32)
        low_rank_product = jnp.dot(rows, adapter_in[replica_index], preferred_element_type=jnp.float32).astype(jnp.bfloat16)
        rotated_mixture = frozen_output * learned_column_scale + ADAPTER_SCALE * jnp.dot(low_rank_product, adapter_up_weight[replica_index], preferred_element_type=jnp.float32)
        value_list.append(rotated_mixture.astype(jnp.bfloat16))
        scale_list.append(lax.optimization_barrier(jnp.sum(output_gradient.astype(jnp.float32) * frozen_output, axis=0)) * shrink_factor)
        output_list.append(jnp.dot(low_rank_product.T, output_gradient, preferred_element_type=jnp.float32) * (ADAPTER_SCALE * shrink_factor))
        backward_rank_term = (jnp.dot(output_gradient, adapter_up_weight[replica_index].T, preferred_element_type=jnp.float32) * ADAPTER_SCALE).astype(jnp.bfloat16)
        in_list.append(jnp.dot(rows.T, backward_rank_term, preferred_element_type=jnp.float32) * shrink_factor)
    next_pending_left = lax.optimization_barrier(jnp.sum(global_left[None] - local_left, axis=0)) / N_REPLICA
    next_pending_right = lax.optimization_barrier(jnp.sum(global_right[None] - local_right, axis=0)) / N_REPLICA
    next_moment_left = MOMENTUM * moment_left + pending_left
    next_moment_right = MOMENTUM * moment_right + pending_right
    next_global_left = global_left - OUTER_RATE * (pending_left + MOMENTUM * next_moment_left)
    next_global_right = global_right - OUTER_RATE * (pending_right + MOMENTUM * next_moment_right)
    return (jnp.concatenate(value_list, axis=0), jnp.stack(in_list), jnp.stack(output_list), jnp.stack(scale_list), next_global_left, next_global_right, next_moment_left, next_moment_right, next_pending_left, next_pending_right)
```

```python
import math

import jax
import jax.numpy as jnp
import numpy as np
from jax import lax
from jax.experimental import pallas as pl
from jax.experimental.pallas import tpu as pltpu
from jax.sharding import PartitionSpec as P

MESH = pl.DeviceIdType.MESH
BF = jnp.bfloat16
F32 = jnp.float32
ADAPTER_SCALE = 2.0
MOMENTUM = 0.9
OUTER_RATE = 0.7
ROWS = 768
NSEM = 160


def hadamard(n):
    i = np.arange(n)
    both = i[:, None] & i[None, :]
    parity = np.zeros((n, n), np.int64)
    for b in range(n.bit_length()):
        parity += (both >> b) & 1
    return (1 - 2 * (parity % 2)).astype(np.float32)


def nt(a, b):
    return lax.dot_general(a, b, (((1,), (1,)), ((), ())), preferred_element_type=F32)


def nn(a, b):
    return jnp.dot(a, b, preferred_element_type=F32)


def body(
    tokens, sign, weight, scale, a_in, up, cot, ll, lr, gl, gr, ml, mr, pend_l, pend_r, had,
    o_val, o_gin, o_gout, o_gs, o_gl, o_gr, o_ml, o_mr, o_pl, o_pr,
    wg, ag, tok, st, sl, g, r1, r2, r3, r4, r5, cotv, upv, acc, low, bt, val, signv, scalev, hadv, wsh,
    go, go_o, go_i, go_x, go_f, gs, gs_o, fl, fr, dl, dr, dl1, dr1, dl2, dr2, gin, gout,
    send, recv, loc, st_sem, sl_sem,
):
    r, f = lax.axis_index("replica"), lax.axis_index("fsdp")
    xh, c = r // 2, r % 2
    y, z, xl = f // 8, (f // 2) % 4, f % 2
    c1, xl1 = 1 - c, 1 - xl
    shrink = 1.0 / math.sqrt(ROWS * 32)

    def dev(dx=0, dy=0, dz=0, dc=0):
        x = (2 * xh + xl + dx + 4) % 4
        return ((x // 2) * 2 + (c + dc) % 2, ((y + dy + 4) % 4) * 8 + ((z + dz + 4) % 4) * 2 + x % 2)

    def xpair():
        return (r, y * 8 + z * 2 + xl1)

    def mod4(v):
        return (v + 4) % 4

    nloc = [0]

    def local(src, dst):
        cp = pltpu.make_async_copy(src, dst, loc.at[nloc[0]])
        nloc[0] += 1
        cp.start()
        return cp

    nrem = [0]
    sent = []

    def push(src, dst, where):
        k = nrem[0]
        nrem[0] += 1
        cp = pltpu.make_async_remote_copy(
            src_ref=src, dst_ref=dst, send_sem=send.at[k], recv_sem=recv.at[k],
            device_id=where, device_id_type=MESH,
        )
        cp.start()
        sent.append(cp)
        return cp

    def row_copy(k):
        rows = pl.ds(pl.multiple_of(k * 48, 48), 48)
        return pltpu.make_async_copy(tokens.at[rows], st.at[k % 2], st_sem.at[k % 2])

    def col_copy(k):
        cols = pl.ds(pl.multiple_of(k * 512, 512), 512)
        return pltpu.make_async_copy(tokens.at[:, cols], sl.at[k % 2], sl_sem.at[k % 2])

    ld_w = local(weight.at[:, pl.ds(pl.multiple_of(c * 512, 512), 512)], wsh)
    ld_h = local(had, hadv)
    ld_a = local(a_in, ag.at[y, z, xl])
    ld_up = local(up, upv)
    ld_cot = local(cot, cotv)
    ld_tok = [local(tokens.at[:, pl.ds(k * 1024, 1024)], tok.at[:, pl.ds(k * 1024, 1024)]) for k in range(8)]
    row_copy(0).start()
    col_copy(0).start()
    ld_s = local(sign, signv)
    ld_sc = local(scale, scalev)
    ld_f = [local(s, fl.at[k]) for k, s in enumerate((ll, gl, ml, pend_l))]
    ld_f += [local(s, fr.at[k]) for k, s in enumerate((lr, gr, mr, pend_r))]

    barrier = pltpu.get_barrier_semaphore()
    peers = [dev(dx=1), dev(dx=-1), dev(dx=2), dev(dy=1), dev(dy=-1), dev(dy=2), dev(dz=1), dev(dz=-1), dev(dz=2), dev(dc=1)]
    for p in peers:
        pl.semaphore_signal(barrier, inc=1, device_id=p, device_id_type=MESH)

    ld_w.wait()
    ld_h.wait()
    w1 = (nn(hadv[...], wsh[...]) * (1.0 / math.sqrt(8192))).astype(BF)
    wg[c, 0, xl, y, z] = w1[:128]
    wg[c, 1, xl, z, y] = w1[128:]
    pl.semaphore_wait(barrier, len(peers))

    pos = [(y, z), (z, y)]

    def out_dev(q, d):
        return dev(dy=d) if q == 0 else dev(dz=d)

    def in_dev(q, d):
        return dev(dz=d) if q == 0 else dev(dy=d)

    w_in, w_out, w_x, w_sib = [{}, {}], [{}, {}], [{}, {}], [{}, {}]

    def wgrp(q, xv, d, ch=None):
        return wg.at[c if ch is None else ch, q, xv, mod4(pos[q][0] + d)]

    def w_in1(q):
        o, i = pos[q]
        ref = wg.at[c, q, xl, o, i]
        for d in (1, -1):
            w_in[q][d] = push(ref, ref, in_dev(q, d))

    def w_in2(q):
        o, i = pos[q]
        for d, h in ((1, 0), (-1, 64)):
            w_in[q][d].wait_recv()
            ref = wg.at[c, q, xl, o, mod4(i - d), pl.ds(h, 64)]
            w_in[q][2 * d] = push(ref, ref, in_dev(q, d))

    def w_share(q, d):
        ref = wgrp(q, xl, d)
        w_x[q][d] = push(ref, ref, dev(dx=-1 if q == 0 else 1))
        w_sib[q][0, d] = push(ref, ref, dev(dc=1))

    def w_out1(q):
        for d in (1, -1):
            w_in[q][2 * d].wait_recv()
        ref = wgrp(q, xl, 0)
        for d in (1, -1):
            w_out[q][d] = push(ref, ref, out_dev(q, d))
        w_share(q, 0)

    def w_out2(q):
        for d, h in ((1, 0), (-1, 2)):
            w_out[q][d].wait_recv()
            ref = wg.at[c, q, xl, mod4(pos[q][0] - d), pl.ds(h, 2)]
            w_out[q][2 * d] = push(ref, ref, out_dev(q, d))
        for d in (1, -1):
            w_share(q, d)

    def w_out3(q):
        for d in (1, -1):
            w_out[q][2 * d].wait_recv()
        w_share(q, 2)

    def w_x1(q, d):
        w_x[q][d].wait_recv()
        ref = wgrp(q, xl1, d)
        w_sib[q][1, d] = push(ref, ref, dev(dc=1))

    a_x, a_i, a_o = {}, [{}, {}], [{}, {}]

    def apiece(q, i, xs=slice(None)):
        return ag.at[y, i, xs, 0] if q == 0 else ag.at[i, z, xs, 1]

    def agrp(q, o, i=slice(None)):
        return ag.at[o, i, :, 0] if q == 0 else ag.at[i, o, :, 1]

    def a_x1():
        ld_a.wait()
        a_x[0] = push(ag.at[y, z, xl], ag.at[y, z, xl], xpair())

    def a_in1(q):
        if q == 0:
            a_x[0].wait_recv()
        ref = apiece(q, pos[q][1])
        for d in (1, -1):
            a_i[q][d] = push(ref, ref, in_dev(q, d))

    def a_in2(q):
        for d, h in ((1, 0), (-1, 1)):
            a_i[q][d].wait_recv()
            ref = apiece(q, mod4(pos[q][1] - d), h)
            a_i[q][2 * d] = push(ref, ref, in_dev(q, d))

    def a_out1(q):
        for d in (1, -1):
            a_i[q][2 * d].wait_recv()
        ref = agrp(q, pos[q][0])
        for d in (1, -1):
            a_o[q][d] = push(ref, ref, out_dev(q, d))

    def a_out2(q):
        for d, h in ((1, 0), (-1, 2)):
            a_o[q][d].wait_recv()
            ref = agrp(q, mod4(pos[q][0] - d), pl.ds(h, 2))
            a_o[q][2 * d] = push(ref, ref, out_dev(q, d))

    def a_out3(q):
        for d in (1, -1):
            a_o[q][2 * d].wait_recv()

    rs = [{}, {}]

    def gidx(q, o, i, xv):
        return (o, i, xv, 0) if q == 0 else (i, o, xv, 1)

    def ggrp(q, o, i=slice(None)):
        return g.at[o, i, :, 0] if q == 0 else g.at[i, o, :, 1]

    def add_to(q, o, i, xv, *terms):
        at = gidx(q, o, i, xv)
        total = g[at].astype(F32)
        for t in terms:
            total = total + t.astype(F32)
        g[at] = total.astype(BF)

    def rs_1(q):
        o = mod4(pos[q][0] + 2)
        for k, (d, h) in enumerate(((1, 0), (-1, 2))):
            rs[q][1, d] = push(ggrp(q, o, pl.ds(h, 2)), r1.at[q, k], out_dev(q, d))

    def rs_2(q):
        for k, (d, h) in enumerate(((1, 0), (-1, 2))):
            rs[q][1, d].wait_recv()
            o = mod4(pos[q][0] + d)

            def one(j, carry, k=k, h=h, o=o):
                add_to(q, o, h + j // 2, j % 2, r1[q, k, j // 2, j % 2])
                return carry

            lax.fori_loop(0, 4, one, 0)
            rs[q][2, d] = push(ggrp(q, o), r2.at[q, k], out_dev(q, d))

    def rs_3(q):
        for d in (1, -1):
            rs[q][2, d].wait_recv()

        def one(j, carry):
            add_to(q, pos[q][0], j // 2, j % 2, r2[q, 0, j // 2, j % 2], r2[q, 1, j // 2, j % 2])
            return carry

        lax.fori_loop(0, 8, one, 0)

    def gpiece(q, i, xs=slice(None)):
        return g.at[y, i, xs, 0] if q == 0 else g.at[i, z, xs, 1]

    def rs_4(q):
        i = mod4(pos[q][1] + 2)
        for k, d in enumerate((1, -1)):
            rs[q][4, d] = push(gpiece(q, i, k), r3.at[q, k], in_dev(q, d))

    def rs_5(q):
        for k, d in enumerate((1, -1)):
            rs[q][4, d].wait_recv()
            i = mod4(pos[q][1] + d)
            add_to(q, pos[q][0], i, k, r3[q, k])
            rs[q][5, d] = push(gpiece(q, i), r4.at[q, k], in_dev(q, d))

    def rs_6(q):
        for d in (1, -1):
            rs[q][5, d].wait_recv()
        for k in range(2):
            add_to(q, pos[q][0], pos[q][1], k, r4[q, 0, k], r4[q, 1, k])
        rs[q][6] = push(gpiece(q, pos[q][1], xl1), r5.at[q], xpair())

    def rs_7(q):
        rs[q][6].wait_recv()
        total = g[gidx(q, pos[q][0], pos[q][1], xl)].astype(F32) + r5[q].astype(F32)
        gin[:, q * 128 : (q + 1) * 128] = (total * shrink).T

    def back():
        ld_up.wait()
        ld_cot.wait()
        for k in range(3):
            bt[:, k * 256 : (k + 1) * 256] = (nt(upv[...], cotv[k * 256 : (k + 1) * 256, :]) * ADAPTER_SCALE).astype(BF)

    def grad_in(ks):
        for k in ks:
            ld_tok[k].wait()

        def one(j, carry):
            cols = pl.ds(pl.multiple_of(j * 256, 256), 256)
            part = nn(bt[...], tok[:, cols]).astype(BF)
            g[j // 8, (j // 2) % 4, j % 2, 0] = part[:128]
            g[j // 8, (j // 2) % 4, j % 2, 1] = part[128:]
            return carry

        lax.fori_loop(ks[0] * 4, ks[-1] * 4 + 4, one, 0)

    def rotate(lo, hi):
        def chunk(k, carry):
            row_copy(k).wait()

            @pl.when(k + 1 < 16)
            def _():
                row_copy(k + 1).start()

            lax.fori_loop(0, 6, lambda j, n: rotate_rows(k, j, n), 0)
            return carry

        lax.fori_loop(lo, hi, chunk, 0)

    def rotate_rows(chunk, k, carry):
        at = pl.multiple_of((k // 2) * 16, 16)
        rows = pl.ds(pl.multiple_of(chunk * 48 + at, 16), 16)
        q = k % 2
        parts = []
        for j in range(32):
            cols = pl.ds(pl.multiple_of(j * 256 + q * 128, 128), 128)
            parts.append(st[chunk % 2, pl.ds(at, 16), cols].astype(F32) * signv[:, cols])
        for b in range(5):
            step = 1 << b
            for j in range(32):
                if not j & step:
                    u, v = parts[j], parts[j + step]
                    parts[j], parts[j + step] = u + v, u - v
        for j in range(32):
            jy, jz, jx = j // 8, (j // 2) % 4, j % 2
            t = q * 32 + jx * 16 + (1 - q) * (jy * 4 + jz) + q * (jz * 4 + jy)
            tok[rows, pl.ds(pl.multiple_of(t * 128, 128), 128)] = parts[j].astype(BF)
        return carry

    def frozen(q, xv, d, ch, first=False):
        o = mod4(pos[q][0] + d)
        at = pl.multiple_of(((q * 2 + xv) * 4 + o) * 512, 512)
        part = nn(tok[:, pl.ds(at, 512)], wg[ch, q, xv, o].reshape(512, 512))
        if first:
            acc[ch] = part
        else:
            acc[ch] += part

    def low_rank():
        def one(k, carry):
            col_copy(k).wait()

            @pl.when(k + 1 < 16)
            def _():
                col_copy(k + 1).start()

            part = nn(sl[k % 2], ag[k // 4, k % 4].reshape(512, 256))
            low[...] = jnp.where(k == 0, part, low[...] + part)
            return carry

        lax.fori_loop(0, 16, one, 0)

    fx = {}

    def frag_1():
        for cp in ld_f:
            cp.wait()
        for buf, d in ((fl, dl), (fr, dr)):
            n = buf.shape[1]
            for h in range(2):
                rows = slice(h * n // 2, (h + 1) * n // 2)
                lv, gv, mv, pv = (buf[k, rows] for k in range(4))
                nm = MOMENTUM * mv + pv
                buf[2, rows] = nm
                buf[0, rows] = gv - OUTER_RATE * (pv + MOMENTUM * nm)
                d[h] = (gv - lv).astype(BF)
        fx["l"] = push(dl.at[c1], dl1, dev(dc=1))
        fx["r"] = push(dr.at[c1], dr1, dev(dc=1))
        return [local(fl.at[0], o_gl), local(fr.at[0], o_gr), local(fl.at[2], o_ml), local(fr.at[2], o_mr)]

    def frag_2():
        for k, d, d1, d2 in (("l", dl, dl1, dl2), ("r", dr, dr1, dr2)):
            fx[k].wait_recv()
            d1[...] = (d1[...].astype(F32) + d[c].astype(F32)).astype(BF)
            fx[k + "x"] = push(d1, d2, dev(dx=2))

    def frag_3():
        for k, d1, d2, buf in (("l", dl1, dl2, fl), ("r", dr1, dr2, fr)):
            fx[k + "x"].wait_recv()
            n = buf.shape[1] // 2
            rows = pl.ds(pl.multiple_of(c * n, n), n)
            buf[3, rows] = (d1[...].astype(F32) + d2[...].astype(F32)) * 0.25
            fx[k + "s"] = push(buf.at[3, rows], buf.at[3, rows], dev(dc=1))

    def frag_4():
        for k in "lr":
            fx[k + "s"].wait_recv()
        return [local(fl.at[3], o_pl), local(fr.at[3], o_pr)]

    gx = {}

    def gout_1():
        lt = low[...].T.astype(BF)
        for q in range(2):
            part = nn(lt, cotv[:, q * 512 : (q + 1) * 512]) * (ADAPTER_SCALE * shrink)
            go[q] = part.astype(BF).reshape(4, 4, 16, 512)
        for q in range(2):
            for k, d in enumerate((1, -1, 2)):
                o = mod4(pos[q][0] + d)
                src = go.at[0, o] if q == 0 else go.at[1, :, o]
                gx[q, 1, k] = push(src, go_o.at[q, k], out_dev(q, d))

    def gout_2():
        for q in range(2):
            for k in range(3):
                gx[q, 1, k].wait_recv()
            own = go[0, y] if q == 0 else go[1, :, z]
            total = own.astype(F32)
            for k in range(3):
                total = total + go_o[q, k].astype(F32)
            go_f[q] = total

    def gout_2s():
        for q in range(2):
            for k, d in enumerate((1, -1, 2)):
                i = mod4(pos[q][1] + d)
                gx[q, 2, k] = push(go_f.at[q, i], go_i.at[q, k], in_dev(q, d))

    def gout_3():
        for q in range(2):
            for k in range(3):
                gx[q, 2, k].wait_recv()
            total = go_f[q, pos[q][1]]
            for k in range(3):
                total = total + go_i[q, k]
            go_x[:, :, q * 512 : (q + 1) * 512] = total.reshape(2, 8, 512)
        gx["x"] = push(go_x.at[xl1], gout.at[1], xpair())

    def gout_4():
        gx["x"].wait_recv()
        gout[0] = go_x[xl] + gout[1]
        return [local(gout.at[0], o_gout)]

    outs = []

    def finish(ch):
        cols = slice(ch * 512, (ch + 1) * 512)
        lowb = low[...].astype(BF)
        sums = jnp.zeros((1, 512), F32)
        for k in range(3):
            rows = slice(k * 256, (k + 1) * 256)
            fo = acc[ch, rows]
            mix = fo * scalev[:, cols] + ADAPTER_SCALE * nn(lowb[rows], upv[:, cols])
            val[rows, cols] = mix.astype(BF)
            sums = sums + jnp.sum(cotv[rows, cols].astype(F32) * fo, axis=0, keepdims=True)
        gs[0:1, cols] = sums * shrink

    sx = {}

    def scale_x():
        sx["x"] = push(gs.at[0:1], gs_o.at[6:7], xpair())

    def scale_i():
        sx["x"].wait_recv()
        gs[1:2] = gs[0:1] + gs_o[6:7]
        for k, d in enumerate((1, -1, 2)):
            sx["i", k] = push(gs.at[1:2], gs_o.at[k : k + 1], dev(dz=d))

    def scale_o():
        for k in range(3):
            sx["i", k].wait_recv()
        gs[2:3] = (gs[1:2] + gs_o[2:3]) + (gs_o[0:1] + gs_o[1:2])
        for k, d in enumerate((1, -1, 2)):
            sx["o", k] = push(gs.at[2:3], gs_o.at[3 + k : 4 + k], dev(dy=d))

    def scale_f():
        for k in range(3):
            sx["o", k].wait_recv()
        gs[3:4] = (gs[2:3] + gs_o[5:6]) + (gs_o[3:4] + gs_o[4:5])
        return [local(gs.at[3:4], o_gs)]

    def both(fn):
        fn(0)
        fn(1)

    both(w_in1)
    a_x1()
    back()
    both(w_in2)
    grad_in([0, 1])
    both(w_out1)
    both(a_in1)
    grad_in([2, 3, 4, 5, 6, 7])
    both(a_in2)
    ld_s.wait()
    outs += frag_1()
    both(rs_1)
    rotate(0, 8)
    frag_2()
    both(a_out1)
    both(w_out2)
    rotate(8, 16)
    both(rs_2)
    for q in range(2):
        w_sib[q][0, 0].wait_recv()
        for ch in range(2):
            frozen(q, xl, 0, ch, first=q == 0)
    frag_3()
    both(a_out2)
    both(w_out3)
    for q in range(2):
        for d in (1, -1):
            w_sib[q][0, d].wait_recv()
            for ch in range(2):
                frozen(q, xl, d, ch)
    for q in range(2):
        w_x1(q, 0)
    both(a_out3)
    low_rank()
    gout_1()
    both(rs_3)
    both(rs_4)
    for q in range(2):
        w_sib[q][0, 2].wait_recv()
        for ch in range(2):
            frozen(q, xl, 2, ch)
    gout_2()
    gout_2s()
    both(rs_5)
    outs += frag_4()
    for d in (1, -1):
        for q in range(2):
            w_x1(q, d)
    for q in range(2):
        w_sib[q][1, 0].wait_recv()
        for ch in range(2):
            frozen(q, xl1, 0, ch)
    gout_3()
    both(rs_6)
    for d in (1, -1):
        for q in range(2):
            w_sib[q][1, d].wait_recv()
            for ch in range(2):
                frozen(q, xl1, d, ch)
    outs += gout_4()
    for q in range(2):
        w_x1(q, 2)
    for q in range(2):
        w_sib[q][1, 2].wait_recv()
        for ch in range(2):
            frozen(q, xl1, 2, ch)
    ld_sc.wait()
    for ch in range(2):
        finish(ch)
    scale_x()
    outs.append(local(val, o_val))
    both(rs_7)
    scale_i()
    outs.append(local(gin, o_gin))
    scale_o()
    outs += scale_f()
    for cp in sent:
        cp.wait_send()
    for cp in outs:
        cp.wait()


def call(*args):
    vm = pltpu.VMEM
    out = [
        jax.ShapeDtypeStruct((ROWS, 1024), BF),
        jax.ShapeDtypeStruct((256, 256), F32),
        jax.ShapeDtypeStruct((8, 1024), F32),
        jax.ShapeDtypeStruct((1, 1024), F32),
        jax.ShapeDtypeStruct((1024, 256), F32),
        jax.ShapeDtypeStruct((32, 1024), F32),
        jax.ShapeDtypeStruct((1024, 256), F32),
        jax.ShapeDtypeStruct((32, 1024), F32),
        jax.ShapeDtypeStruct((1024, 256), F32),
        jax.ShapeDtypeStruct((32, 1024), F32),
    ]
    scratch = [
        vm((2, 2, 2, 4, 4, 128, 512), BF),
        vm((4, 4, 2, 2, 128, 256), BF),
        vm((ROWS, 8192), BF),
        vm((2, 48, 8192), BF),
        vm((2, ROWS, 512), BF),
        vm((4, 4, 2, 2, 128, 256), BF),
        vm((2, 2, 2, 2, 128, 256), BF),
        vm((2, 2, 4, 2, 128, 256), BF),
        vm((2, 2, 128, 256), BF),
        vm((2, 2, 2, 128, 256), BF),
        vm((2, 128, 256), BF),
        vm((ROWS, 1024), BF),
        vm((256, 1024), BF),
        vm((2, ROWS, 512), F32),
        vm((ROWS, 256), F32),
        vm((256, ROWS), BF),
        vm((ROWS, 1024), BF),
        vm((1, 8192), F32),
        vm((1, 1024), F32),
        vm((256, 256), BF),
        vm((256, 512), BF),
        vm((2, 4, 4, 16, 512), BF),
        vm((2, 3, 4, 16, 512), BF),
        vm((2, 3, 16, 512), F32),
        vm((2, 8, 1024), F32),
        vm((2, 4, 16, 512), F32),
        vm((8, 1024), F32),
        vm((8, 1024), F32),
        vm((4, 1024, 256), F32),
        vm((4, 32, 1024), F32),
        vm((2, 512, 256), BF),
        vm((2, 16, 1024), BF),
        vm((512, 256), BF),
        vm((16, 1024), BF),
        vm((512, 256), BF),
        vm((16, 1024), BF),
        vm((256, 256), F32),
        vm((2, 8, 1024), F32),
        pltpu.SemaphoreType.DMA((NSEM,)),
        pltpu.SemaphoreType.DMA((NSEM,)),
        pltpu.SemaphoreType.DMA((40,)),
        pltpu.SemaphoreType.DMA((2,)),
        pltpu.SemaphoreType.DMA((2,)),
    ]
    hbm = pl.BlockSpec(memory_space=pl.ANY)
    return pl.pallas_call(
        body,
        name="step",
        out_shape=out,
        in_specs=[hbm] * len(args),
        out_specs=[hbm] * len(out),
        scratch_shapes=scratch,
        compiler_params=pltpu.CompilerParams(
            collective_id=0, has_side_effects=True, vmem_limit_bytes=64 * 1024 * 1024
        ),
        cost_estimate=pl.CostEstimate(flops=23_000_000_000, bytes_accessed=30_000_000, transcendentals=0),
    )(*args)


def per_device(
    tokens, sign_bits, base_weight, learned_column_scale, adapter_in, adapter_up_weight, out_cotangent,
    local_left, local_right, global_left, global_right, moment_left, moment_right, pending_left, pending_right,
):
    sign = (1 - 2 * sign_bits).astype(F32).reshape(1, 8192)
    left = [a.reshape(1024, 256) for a in (local_left, global_left, moment_left, pending_left)]
    right = [a.reshape(32, 1024) for a in (local_right, global_right, moment_right, pending_right)]
    pairs = [a for pair in zip(left, right) for a in pair]
    had = jnp.asarray(hadamard(256), BF)
    out = call(
        tokens, sign, base_weight, learned_column_scale.reshape(1, 1024),
        adapter_in.reshape(2, 128, 256), adapter_up_weight.reshape(256, 1024), out_cotangent, *pairs, had,
    )
    val, gin, gout, gs, gl, gr, ml, mr, pdl, pdr = out
    return (
        val, gin[None], gout[None], gs,
        gl.reshape(4, 256, 256), gr.reshape(4, 8, 1024), ml.reshape(4, 256, 256), mr.reshape(4, 8, 1024),
        pdl.reshape(4, 256, 256), pdr.reshape(4, 8, 1024),
    )


def solution(mesh):
    rows, frag = P(("replica", "fsdp"), None), P(None, "fsdp", None)
    return jax.shard_map(
        per_device,
        mesh=mesh,
        in_specs=(
            rows, P(), P("fsdp", None), P(), P("replica", "fsdp", None), P("replica", None, None), rows,
            P("replica", None, "fsdp", None), P("replica", None, "fsdp", None),
        ) + (frag,) * 6,
        out_specs=(rows, P("replica", "fsdp", None), P("replica", "fsdp", None), P("replica", None)) + (frag,) * 6,
        check_vma=False,
    )
```

```python
import math

import jax
import jax.numpy as jnp
from jax import lax
from jax.experimental import pallas as pl
from jax.experimental.pallas import tpu as pltpu
from jax.sharding import PartitionSpec as P

MESH = pl.DeviceIdType.MESH
BF = jnp.bfloat16
F32 = jnp.float32
ADAPTER_SCALE = 2.0
MOMENTUM = 0.9
OUTER_RATE = 0.7
ROWS = 768
NSEM = 192


def nt(a, b):
    return lax.dot_general(a, b, (((1,), (1,)), ((), ())), preferred_element_type=F32)


def nn(a, b):
    return jnp.dot(a, b, preferred_element_type=F32)


def body(
    tokens, sign, weight, scale, a_in, up, cot, ll, lr, gl, gr, ml, mr, pend_l, pend_r,
    o_val, o_gin, o_gout, o_gs, o_gl, o_gr, o_ml, o_mr, o_pl, o_pr,
    wg, ag, tok, st, sgn, sl, g, r1, r2, r3, r4, r5, cotv, upv, acc, low, bt, val, signv, scalev, wsh,
    go, go_o, go_i, go_x, go_f, gs, gs_o, fl, fr, dl, dr, dl1, dr1, dl2, dr2, gin, gout,
    send, recv, loc, sl_sem,
):
    r, f = lax.axis_index("replica"), lax.axis_index("fsdp")
    xh, c = r // 2, r % 2
    y, z, xl = f // 8, (f // 2) % 4, f % 2
    c1, xl1 = 1 - c, 1 - xl
    shrink = 1.0 / math.sqrt(ROWS * 32)

    def dev(dx=0, dy=0, dz=0, dc=0):
        x = (2 * xh + xl + dx + 4) % 4
        return ((x // 2) * 2 + (c + dc) % 2, ((y + dy + 4) % 4) * 8 + ((z + dz + 4) % 4) * 2 + x % 2)

    def xpair():
        return (r, y * 8 + z * 2 + xl1)

    def mod4(v):
        return (v + 4) % 4

    nloc = [0]

    def local(src, dst):
        cp = pltpu.make_async_copy(src, dst, loc.at[nloc[0]])
        nloc[0] += 1
        cp.start()
        return cp

    nrem = [0]
    sent = []

    def push(src, dst, where):
        k = nrem[0]
        nrem[0] += 1
        cp = pltpu.make_async_remote_copy(
            src_ref=src, dst_ref=dst, send_sem=send.at[k], recv_sem=recv.at[k],
            device_id=where, device_id_type=MESH,
        )
        cp.start()
        sent.append(cp)
        return cp

    def col_copies(k):
        cols = pl.ds(pl.multiple_of(k * 1024, 1024), 1024)
        return [
            pltpu.make_async_copy(
                tokens.at[pl.ds(n * 192, 192), cols], sl.at[k % 2, pl.ds(n * 192, 192)], sl_sem.at[k % 2, n]
            )
            for n in range(4)
        ]

    ld_w = local(weight.at[:, pl.ds(pl.multiple_of(c * 512, 512), 512)], wsh)
    ld_a = local(a_in, ag.at[y, z, xl])
    ld_up = local(up, upv)
    ld_cot = local(cot, cotv)
    ld_tok = [local(tokens.at[:, pl.ds(k * 1024, 1024)], tok.at[:, pl.ds(k * 1024, 1024)]) for k in range(8)]
    ld_s = local(sign, signv)
    ld_sc = local(scale, scalev)
    ld_f = [local(s, fl.at[k]) for k, s in enumerate((ll, gl, ml, pend_l))]
    ld_f += [local(s, fr.at[k]) for k, s in enumerate((lr, gr, mr, pend_r))]

    barrier = pltpu.get_barrier_semaphore()
    peers = [dev(dx=1), dev(dx=-1), dev(dx=2), dev(dy=1), dev(dy=-1), dev(dy=2), dev(dz=1), dev(dz=-1), dev(dz=2), dev(dc=1)]
    for p in peers:
        pl.semaphore_signal(barrier, inc=1, device_id=p, device_id_type=MESH)

    ld_w.wait()
    both_bits = lax.broadcasted_iota(jnp.int32, (256, 256), 0) & lax.broadcasted_iota(jnp.int32, (256, 256), 1)
    for b in (4, 2, 1):
        both_bits = both_bits ^ (both_bits >> b)
    had = (1 - 2 * (both_bits & 1)).astype(F32).astype(BF)
    w1 = (nn(had, wsh[...]) * (1.0 / math.sqrt(8192))).astype(BF)
    wg[c, 0, xl, y, z] = w1[:128]
    wg[c, 1, xl, z, y] = w1[128:]
    pl.semaphore_wait(barrier, len(peers))

    pos = [(y, z), (z, y)]

    def out_dev(q, d):
        return dev(dy=d) if q == 0 else dev(dz=d)

    def in_dev(q, d):
        return dev(dz=d) if q == 0 else dev(dy=d)

    w_in, w_po, w_pf, w_px, w_sib = ([{}, {}] for _ in range(5))

    def wp(q, do, di):
        o, i = pos[q]
        return wg.at[c, q, xl, mod4(o + do), mod4(i + di)]

    def x_dev(q):
        return dev(dx=-1 if q == 0 else 1)

    def w_out(q, di):
        ref = wp(q, 0, di)
        for d in (1, -1):
            w_po[q][di, d] = push(ref, ref, out_dev(q, d))

    def w_cross(q, do, di):
        ref = wp(q, do, di)
        w_px[q][do, di] = push(ref, ref, x_dev(q))

    def w_share(q, far, do):
        ref = wg.at[c, q, xl1 if far else xl, mod4(pos[q][0] + do)]
        w_sib[q][far, do] = push(ref, ref, dev(dc=1))

    def w_1(q):
        ref = wp(q, 0, 0)
        for d in (1, -1):
            w_in[q][d] = push(ref, ref, in_dev(q, d))
        w_out(q, 0)
        w_cross(q, 0, 0)

    def w_2(q):
        for d, h in ((1, 0), (-1, 64)):
            w_in[q][d].wait_recv()
            o, i = pos[q]
            ref = wg.at[c, q, xl, o, mod4(i - d), pl.ds(h, 64)]
            w_in[q][2 * d] = push(ref, ref, in_dev(q, d))
            w_out(q, -d)
            w_cross(q, 0, -d)

    def w_fwd(q, d, di):
        ref = wp(q, -d, di)
        w_pf[q][di] = push(ref, ref, out_dev(q, d))

    def w_got(q, d, di):
        w_po[q][di, d].wait_recv()
        w_cross(q, -d, di)
        if (d == 1) == (di in (0, 1)):
            w_fwd(q, d, di)

    def w_3(q):
        for d in (1, -1):
            w_got(q, d, 0)
        for d in (1, -1):
            w_in[q][2 * d].wait_recv()
        w_out(q, 2)
        w_cross(q, 0, 2)
        w_share(q, 0, 0)

    def w_4(q):
        for di in (1, -1):
            for d in (1, -1):
                w_got(q, d, di)

    def w_5(q):
        for d in (1, -1):
            w_got(q, d, 2)
            w_share(q, 0, -d)

    def w_6(q):
        for di in (0, 1, -1, 2):
            w_pf[q][di].wait_recv()
            w_cross(q, 2, di)
        w_share(q, 0, 2)

    def w_7(q, do):
        for di in (0, 1, -1, 2):
            w_px[q][do, di].wait_recv()
        w_share(q, 1, do)

    a_x, a_i, a_o = {}, [{}, {}], [{}, {}]

    def apiece(q, i, xs=slice(None)):
        return ag.at[y, i, xs, 0] if q == 0 else ag.at[i, z, xs, 1]

    def agrp(q, o, i=slice(None)):
        return ag.at[o, i, :, 0] if q == 0 else ag.at[i, o, :, 1]

    def a_x1():
        ld_a.wait()
        a_x[0] = push(ag.at[y, z, xl], ag.at[y, z, xl], xpair())

    def a_in1(q):
        if q == 0:
            a_x[0].wait_recv()
        ref = apiece(q, pos[q][1])
        for d in (1, -1):
            a_i[q][d] = push(ref, ref, in_dev(q, d))

    def a_in2(q):
        for d, h in ((1, 0), (-1, 1)):
            a_i[q][d].wait_recv()
            ref = apiece(q, mod4(pos[q][1] - d), h)
            a_i[q][2 * d] = push(ref, ref, in_dev(q, d))

    def a_out1(q):
        for d in (1, -1):
            a_i[q][2 * d].wait_recv()
        ref = agrp(q, pos[q][0])
        for d in (1, -1):
            a_o[q][d] = push(ref, ref, out_dev(q, d))

    def a_out2(q):
        for d, h in ((1, 0), (-1, 2)):
            a_o[q][d].wait_recv()
            ref = agrp(q, mod4(pos[q][0] - d), pl.ds(h, 2))
            a_o[q][2 * d] = push(ref, ref, out_dev(q, d))

    def a_out3(q):
        for d in (1, -1):
            a_o[q][2 * d].wait_recv()

    rs = [{}, {}]

    def gidx(q, o, i, xv):
        return (o, i, xv, 0) if q == 0 else (i, o, xv, 1)

    def ggrp(q, o, i=slice(None)):
        return g.at[o, i, :, 0] if q == 0 else g.at[i, o, :, 1]

    def add_to(q, o, i, xv, *terms):
        at = gidx(q, o, i, xv)
        total = g[at].astype(F32)
        for t in terms:
            total = total + t.astype(F32)
        g[at] = total.astype(BF)

    def rs_1(q):
        o = mod4(pos[q][0] + 2)
        for k, (d, h) in enumerate(((1, 0), (-1, 2))):
            rs[q][1, d] = push(ggrp(q, o, pl.ds(h, 2)), r1.at[q, k], out_dev(q, d))

    def rs_2(q):
        for k, (d, h) in enumerate(((1, 0), (-1, 2))):
            rs[q][1, d].wait_recv()
            o = mod4(pos[q][0] + d)

            def one(j, carry, k=k, h=h, o=o):
                add_to(q, o, h + j // 2, j % 2, r1[q, k, j // 2, j % 2])
                return carry

            lax.fori_loop(0, 4, one, 0)
            rs[q][2, d] = push(ggrp(q, o), r2.at[q, k], out_dev(q, d))

    def rs_3(q):
        for d in (1, -1):
            rs[q][2, d].wait_recv()

        def one(j, carry):
            add_to(q, pos[q][0], j // 2, j % 2, r2[q, 0, j // 2, j % 2], r2[q, 1, j // 2, j % 2])
            return carry

        lax.fori_loop(0, 8, one, 0)

    def gpiece(q, i, xs=slice(None)):
        return g.at[y, i, xs, 0] if q == 0 else g.at[i, z, xs, 1]

    def rs_4(q):
        i = mod4(pos[q][1] + 2)
        for k, d in enumerate((1, -1)):
            rs[q][4, d] = push(gpiece(q, i, k), r3.at[q, k], in_dev(q, d))

    def rs_5(q):
        for k, d in enumerate((1, -1)):
            rs[q][4, d].wait_recv()
            i = mod4(pos[q][1] + d)
            add_to(q, pos[q][0], i, k, r3[q, k])
            rs[q][5, d] = push(gpiece(q, i), r4.at[q, k], in_dev(q, d))

    def rs_6(q):
        for d in (1, -1):
            rs[q][5, d].wait_recv()
        for k in range(2):
            add_to(q, pos[q][0], pos[q][1], k, r4[q, 0, k], r4[q, 1, k])
        rs[q][6] = push(gpiece(q, pos[q][1], xl1), r5.at[q], xpair())

    def rs_7(q):
        rs[q][6].wait_recv()
        total = g[gidx(q, pos[q][0], pos[q][1], xl)].astype(F32) + r5[q].astype(F32)
        gin[:, q * 128 : (q + 1) * 128] = (total * shrink).T

    def back():
        ld_up.wait()
        ld_cot.wait()
        for k in range(3):
            bt[:, k * 256 : (k + 1) * 256] = (nt(upv[...], cotv[k * 256 : (k + 1) * 256, :]) * ADAPTER_SCALE).astype(BF)

    def grad_in(ks):
        for k in ks:
            ld_tok[k].wait()

        def one(j, carry):
            cols = pl.ds(pl.multiple_of(j * 1024, 1024), 1024)
            part = nn(bt[...], tok[:, cols]).astype(BF)
            for n in range(4):
                for q in range(2):
                    g[j // 2, (j % 2) * 2 + n // 2, n % 2, q] = part[q * 128 : q * 128 + 128, n * 256 : n * 256 + 256]
            return carry

        lax.fori_loop(ks[0], ks[-1] + 1, one, 0)

    def signs():
        ld_s.wait()

        def one(k, carry):
            cols = pl.ds(pl.multiple_of(k * 1024, 1024), 1024)
            flip = (1 - 2 * signv[:, cols]).astype(F32)
            sgn[:, cols] = jnp.broadcast_to(flip, (16, 1024)).astype(BF)
            return carry

        lax.fori_loop(0, 8, one, 0)

    def rotate(lo, hi):
        def one(k, carry):
            rows = pl.ds(pl.multiple_of(k * 16, 16), 16)
            st[...] = tok[rows] * sgn[...]
            for q in range(2):
                parts = [st[:, j * 256 + q * 128 : j * 256 + q * 128 + 128] for j in range(32)]
                for b in range(5):
                    step = 1 << b
                    for j in range(32):
                        if not j & step:
                            u, v = parts[j], parts[j + step]
                            parts[j], parts[j + step] = u + v, u - v
                for j in range(32):
                    jy, jz, jx = j // 8, (j // 2) % 4, j % 2
                    t = q * 32 + jx * 16 + (1 - q) * (jy * 4 + jz) + q * (jz * 4 + jy)
                    tok[rows, t * 128 : t * 128 + 128] = parts[j]
            return carry

        lax.fori_loop(lo, hi, one, 0)

    def frozen(q, xv, d, ch, first=False):
        o = mod4(pos[q][0] + d)
        at = pl.multiple_of(((q * 2 + xv) * 4 + o) * 512, 512)
        part = nn(tok[:, pl.ds(at, 512)], wg[ch, q, xv, o].reshape(512, 512))
        if first:
            acc[ch] = part
        else:
            acc[ch] += part

    def low_start():
        for cp in col_copies(0) + col_copies(1):
            cp.start()

    def low_rank(lo, hi):
        def one(k, carry):
            for cp in col_copies(k):
                cp.wait()
            part = nn(sl[k % 2], ag[k // 2, pl.ds((k % 2) * 2, 2)].reshape(1024, 256))
            low[...] = jnp.where(k == 0, part, low[...] + part)

            @pl.when(k + 2 < 8)
            def _():
                for cp in col_copies(k + 2):
                    cp.start()

            return carry

        lax.fori_loop(lo, hi, one, 0)

    fx = {}

    def frag_1():
        for cp in ld_f:
            cp.wait()
        for buf, d in ((fl, dl), (fr, dr)):
            n = buf.shape[1]
            for h in range(2):
                rows = slice(h * n // 2, (h + 1) * n // 2)
                lv, gv, mv, pv = (buf[k, rows] for k in range(4))
                nm = MOMENTUM * mv + pv
                buf[2, rows] = nm
                buf[0, rows] = gv - OUTER_RATE * (pv + MOMENTUM * nm)
                d[h] = (gv - lv).astype(BF)
        fx["l"] = push(dl.at[c1], dl1, dev(dc=1))
        fx["r"] = push(dr.at[c1], dr1, dev(dc=1))
        return [local(fl.at[0], o_gl), local(fr.at[0], o_gr), local(fl.at[2], o_ml), local(fr.at[2], o_mr)]

    def frag_2():
        for k, d, d1, d2 in (("l", dl, dl1, dl2), ("r", dr, dr1, dr2)):
            fx[k].wait_recv()
            d1[...] = (d1[...].astype(F32) + d[c].astype(F32)).astype(BF)
            fx[k + "x"] = push(d1, d2, dev(dx=2))

    def frag_3():
        for k, d1, d2, buf in (("l", dl1, dl2, fl), ("r", dr1, dr2, fr)):
            fx[k + "x"].wait_recv()
            n = buf.shape[1] // 2
            rows = pl.ds(pl.multiple_of(c * n, n), n)
            buf[3, rows] = (d1[...].astype(F32) + d2[...].astype(F32)) * 0.25
            fx[k + "s"] = push(buf.at[3, rows], buf.at[3, rows], dev(dc=1))

    def frag_4():
        for k in "lr":
            fx[k + "s"].wait_recv()
        return [local(fl.at[3], o_pl), local(fr.at[3], o_pr)]

    gx = {}

    def gout_1():
        lt = low[...].T.astype(BF)
        for q in range(2):
            part = nn(lt, cotv[:, q * 512 : (q + 1) * 512]) * (ADAPTER_SCALE * shrink)
            go[q] = part.astype(BF).reshape(4, 4, 16, 512)
        for q in range(2):
            for k, d in enumerate((1, -1, 2)):
                o = mod4(pos[q][0] + d)
                src = go.at[0, o] if q == 0 else go.at[1, :, o]
                gx[q, 1, k] = push(src, go_o.at[q, k], out_dev(q, d))

    def gout_2():
        for q in range(2):
            for k in range(3):
                gx[q, 1, k].wait_recv()
            own = go[0, y] if q == 0 else go[1, :, z]
            total = own.astype(F32)
            for k in range(3):
                total = total + go_o[q, k].astype(F32)
            go_f[q] = total

    def gout_2s():
        for q in range(2):
            for k, d in enumerate((1, -1, 2)):
                i = mod4(pos[q][1] + d)
                gx[q, 2, k] = push(go_f.at[q, i], go_i.at[q, k], in_dev(q, d))

    def gout_3():
        for q in range(2):
            for k in range(3):
                gx[q, 2, k].wait_recv()
            total = go_f[q, pos[q][1]]
            for k in range(3):
                total = total + go_i[q, k]
            go_x[:, :, q * 512 : (q + 1) * 512] = total.reshape(2, 8, 512)
        gx["x"] = push(go_x.at[xl1], gout.at[1], xpair())

    def gout_4():
        gx["x"].wait_recv()
        gout[0] = go_x[xl] + gout[1]
        return [local(gout.at[0], o_gout)]

    outs = []

    def finish(ch):
        cols = slice(ch * 512, (ch + 1) * 512)
        lowb = low[...].astype(BF)
        sums = jnp.zeros((1, 512), F32)
        for k in range(3):
            rows = slice(k * 256, (k + 1) * 256)
            fo = acc[ch, rows]
            mix = fo * scalev[:, cols] + ADAPTER_SCALE * nn(lowb[rows], upv[:, cols])
            val[rows, cols] = mix.astype(BF)
            sums = sums + jnp.sum(cotv[rows, cols].astype(F32) * fo, axis=0, keepdims=True)
        gs[0:1, cols] = sums * shrink

    sx = {}

    def scale_x():
        sx["x"] = push(gs.at[0:1], gs_o.at[6:7], xpair())

    def scale_i():
        sx["x"].wait_recv()
        gs[1:2] = gs[0:1] + gs_o[6:7]
        for k, d in enumerate((1, -1, 2)):
            sx["i", k] = push(gs.at[1:2], gs_o.at[k : k + 1], dev(dz=d))

    def scale_o():
        for k in range(3):
            sx["i", k].wait_recv()
        gs[2:3] = (gs[1:2] + gs_o[2:3]) + (gs_o[0:1] + gs_o[1:2])
        for k, d in enumerate((1, -1, 2)):
            sx["o", k] = push(gs.at[2:3], gs_o.at[3 + k : 4 + k], dev(dy=d))

    def scale_f():
        for k in range(3):
            sx["o", k].wait_recv()
        gs[3:4] = (gs[2:3] + gs_o[5:6]) + (gs_o[3:4] + gs_o[4:5])
        return [local(gs.at[3:4], o_gs)]

    def both(fn):
        fn(0)
        fn(1)

    def use(far, do):
        for q in range(2):
            w_sib[q][far, do].wait_recv()
            for ch in range(2):
                frozen(q, xl1 if far else xl, do, ch, first=far == 0 and do == 0 and q == 0)

    both(w_1)
    a_x1()
    back()
    grad_in([0, 1])
    both(w_2)
    grad_in([2, 3, 4, 5])
    both(a_in1)
    both(w_3)
    grad_in([6, 7])
    signs()
    rotate(0, 24)
    both(w_4)
    both(a_in2)
    rotate(24, 48)
    both(w_5)
    both(a_out1)
    low_start()
    outs += frag_1()
    use(0, 0)
    both(w_6)
    both(rs_1)
    use(0, 1)
    use(0, -1)
    for q in range(2):
        w_7(q, 0)
    frag_2()
    use(0, 2)
    both(a_out2)
    use(1, 0)
    both(rs_2)
    for do in (1, -1):
        for q in range(2):
            w_7(q, do)
    both(a_out3)
    low_rank(0, 8)
    gout_1()
    both(rs_3)
    both(rs_4)
    use(1, 1)
    use(1, -1)
    frag_3()
    gout_2()
    gout_2s()
    both(rs_5)
    for q in range(2):
        w_7(q, 2)
    both(rs_6)
    outs += frag_4()
    use(1, 2)
    ld_sc.wait()
    for ch in range(2):
        finish(ch)
    scale_x()
    outs.append(local(val, o_val))
    gout_3()
    scale_i()
    both(rs_7)
    outs.append(local(gin, o_gin))
    scale_o()
    outs += gout_4()
    outs += scale_f()
    for cp in sent:
        cp.wait_send()
    for cp in outs:
        cp.wait()


def call(*args):
    vm = pltpu.VMEM
    out = [
        jax.ShapeDtypeStruct((ROWS, 1024), BF),
        jax.ShapeDtypeStruct((256, 256), F32),
        jax.ShapeDtypeStruct((8, 1024), F32),
        jax.ShapeDtypeStruct((1, 1024), F32),
        jax.ShapeDtypeStruct((1024, 256), F32),
        jax.ShapeDtypeStruct((32, 1024), F32),
        jax.ShapeDtypeStruct((1024, 256), F32),
        jax.ShapeDtypeStruct((32, 1024), F32),
        jax.ShapeDtypeStruct((1024, 256), F32),
        jax.ShapeDtypeStruct((32, 1024), F32),
    ]
    scratch = [
        vm((2, 2, 2, 4, 4, 128, 512), BF),
        vm((4, 4, 2, 2, 128, 256), BF),
        vm((ROWS, 8192), BF),
        vm((16, 8192), BF),
        vm((16, 8192), BF),
        vm((2, ROWS, 1024), BF),
        vm((4, 4, 2, 2, 128, 256), BF),
        vm((2, 2, 2, 2, 128, 256), BF),
        vm((2, 2, 4, 2, 128, 256), BF),
        vm((2, 2, 128, 256), BF),
        vm((2, 2, 2, 128, 256), BF),
        vm((2, 128, 256), BF),
        vm((ROWS, 1024), BF),
        vm((256, 1024), BF),
        vm((2, ROWS, 512), F32),
        vm((ROWS, 256), F32),
        vm((256, ROWS), BF),
        vm((ROWS, 1024), BF),
        vm((1, 8192), jnp.int32),
        vm((1, 1024), F32),
        vm((256, 512), BF),
        vm((2, 4, 4, 16, 512), BF),
        vm((2, 3, 4, 16, 512), BF),
        vm((2, 3, 16, 512), F32),
        vm((2, 8, 1024), F32),
        vm((2, 4, 16, 512), F32),
        vm((8, 1024), F32),
        vm((8, 1024), F32),
        vm((4, 1024, 256), F32),
        vm((4, 32, 1024), F32),
        vm((2, 512, 256), BF),
        vm((2, 16, 1024), BF),
        vm((512, 256), BF),
        vm((16, 1024), BF),
        vm((512, 256), BF),
        vm((16, 1024), BF),
        vm((256, 256), F32),
        vm((2, 8, 1024), F32),
        pltpu.SemaphoreType.DMA((NSEM,)),
        pltpu.SemaphoreType.DMA((NSEM,)),
        pltpu.SemaphoreType.DMA((40,)),
        pltpu.SemaphoreType.DMA((2, 4)),
    ]
    hbm = pl.BlockSpec(memory_space=pl.ANY)
    return pl.pallas_call(
        body,
        name="step",
        out_shape=out,
        in_specs=[hbm] * len(args),
        out_specs=[hbm] * len(out),
        scratch_shapes=scratch,
        compiler_params=pltpu.CompilerParams(
            collective_id=0, has_side_effects=True, vmem_limit_bytes=64 * 1024 * 1024
        ),
        cost_estimate=pl.CostEstimate(flops=23_000_000_000, bytes_accessed=30_000_000, transcendentals=0),
    )(*args)


def hand_over(refs):
    n = len(refs)

    def copy_all(*args):
        src, dst, held = args[:n], args[n : 2 * n], args[2 * n : 3 * n]
        sem_in, sem_out = args[3 * n :]
        into = [pltpu.make_async_copy(a, b, sem_in.at[k]) for k, (a, b) in enumerate(zip(src, held))]
        away = [pltpu.make_async_copy(a, b, sem_out.at[k]) for k, (a, b) in enumerate(zip(held, dst))]
        for cp in into:
            cp.start()
        for a, b in zip(into, away):
            a.wait()
            b.start()
        for cp in away:
            cp.wait()

    hbm = pl.BlockSpec(memory_space=pl.ANY)
    return pl.pallas_call(
        copy_all,
        name="hand_over",
        out_shape=[jax.ShapeDtypeStruct(a.shape, a.dtype) for a in refs],
        in_specs=[hbm] * n,
        out_specs=[hbm] * n,
        scratch_shapes=[pltpu.VMEM(a.shape, a.dtype) for a in refs]
        + [pltpu.SemaphoreType.DMA((n,)), pltpu.SemaphoreType.DMA((n,))],
        compiler_params=pltpu.CompilerParams(vmem_limit_bytes=60 * 1024 * 1024),
    )(*refs)


def per_device(
    tokens, sign_bits, base_weight, learned_column_scale, adapter_in, adapter_up_weight, out_cotangent,
    local_left, local_right, global_left, global_right, moment_left, moment_right, pending_left, pending_right,
):
    left = [a.reshape(1024, 256) for a in (local_left, global_left, moment_left, pending_left)]
    right = [a.reshape(32, 1024) for a in (local_right, global_right, moment_right, pending_right)]
    pairs = [a for pair in zip(left, right) for a in pair]
    out = call(
        tokens, sign_bits.reshape(1, 8192), base_weight, learned_column_scale.reshape(1, 1024),
        adapter_in.reshape(2, 128, 256), adapter_up_weight.reshape(256, 1024), out_cotangent, *pairs,
    )
    val, gin, gout, gs, gl, gr, ml, mr, pdl, pdr = out
    return hand_over((
        val, gin[None], gout[None], gs,
        gl.reshape(4, 256, 256), gr.reshape(4, 8, 1024), ml.reshape(4, 256, 256), mr.reshape(4, 8, 1024),
        pdl.reshape(4, 256, 256), pdr.reshape(4, 8, 1024),
    ))


def solution(mesh):
    rows, frag = P(("replica", "fsdp"), None), P(None, "fsdp", None)
    return jax.shard_map(
        per_device,
        mesh=mesh,
        in_specs=(
            rows, P(), P("fsdp", None), P(), P("replica", "fsdp", None), P("replica", None, None), rows,
            P("replica", None, "fsdp", None), P("replica", None, "fsdp", None),
        ) + (frag,) * 6,
        out_specs=(rows, P("replica", "fsdp", None), P("replica", "fsdp", None), P("replica", None)) + (frag,) * 6,
        check_vma=False,
    )
```

```python
import math

import jax
import jax.numpy as jnp
from jax import lax
from jax.experimental import pallas as pl
from jax.experimental.pallas import tpu as pltpu
from jax.sharding import PartitionSpec as P

MESH = pl.DeviceIdType.MESH
BF = jnp.bfloat16
F32 = jnp.float32
ADAPTER_SCALE = 2.0
MOMENTUM = 0.9
OUTER_RATE = 0.7
ROWS = 768
NSEM = 224


def nt(a, b):
    return lax.dot_general(a, b, (((1,), (1,)), ((), ())), preferred_element_type=F32)


def nn(a, b):
    return jnp.dot(a, b, preferred_element_type=F32)


def body(
    tokens, sign, weight, scale, a_in, up, cot, ll, lr, gl, gr, ml, mr, pend_l, pend_r,
    o_val, o_gin, o_gout, o_gs, o_gl, o_gr, o_ml, o_mr, o_pl, o_pr,
    wg, ag, tok, st, sgn, sl, g, r1, r2, r3, r4, r5, cotv, upv, acc, low, bt, val, signv, scalev, wsh,
    go, go_o, go_i, go_x, go_f, gs, gs_o, fl, fr, dl, dr, dl1, dr1, dl2, dr2, gin_t, gin, gout,
    send, recv, loc, sl_sem,
):
    r, f = lax.axis_index("replica"), lax.axis_index("fsdp")
    xh, c = r // 2, r % 2
    y, z, xl = f // 8, (f // 2) % 4, f % 2
    c1, xl1 = 1 - c, 1 - xl
    shrink = 1.0 / math.sqrt(ROWS * 32)

    def dev(dx=0, dy=0, dz=0, dc=0):
        x = (2 * xh + xl + dx + 4) % 4
        return ((x // 2) * 2 + (c + dc) % 2, ((y + dy + 4) % 4) * 8 + ((z + dz + 4) % 4) * 2 + x % 2)

    def xpair():
        return (r, y * 8 + z * 2 + xl1)

    def mod4(v):
        return (v + 4) % 4

    barrier = pltpu.get_barrier_semaphore()
    peers = [dev(dx=1), dev(dx=-1), dev(dx=2), dev(dy=1), dev(dy=-1), dev(dy=2), dev(dz=1), dev(dz=-1), dev(dz=2), dev(dc=1)]
    for p in peers:
        pl.semaphore_signal(barrier, inc=1, device_id=p, device_id_type=MESH)

    nloc = [0]

    def local(src, dst):
        cp = pltpu.make_async_copy(src, dst, loc.at[nloc[0]])
        nloc[0] += 1
        cp.start()
        return cp

    nrem = [0]
    sent = []

    def push(src, dst, where):
        k = nrem[0]
        nrem[0] += 1
        cp = pltpu.make_async_remote_copy(
            src_ref=src, dst_ref=dst, send_sem=send.at[k], recv_sem=recv.at[k],
            device_id=where, device_id_type=MESH,
        )
        cp.start()
        sent.append(cp)
        return cp

    def low_chunk(k):
        n = k % 4
        return mod4(y + (n ^ (n // 2))), (z // 2 + k // 4) % 2

    def col_copies(k):
        cy, cz = low_chunk(k)
        cols = pl.ds(pl.multiple_of(cy * 2048 + cz * 1024, 1024), 1024)
        return [
            pltpu.make_async_copy(
                tokens.at[pl.ds(n * 192, 192), cols], sl.at[k % 2, pl.ds(n * 192, 192)], sl_sem.at[k % 2, n]
            )
            for n in range(4)
        ]

    ld_w = local(weight.at[:, pl.ds(pl.multiple_of(c * 512, 512), 512)], wsh)
    ld_up = local(up, upv)
    ld_a = local(a_in, ag.at[y, z, xl])
    ld_cot = local(cot, cotv)
    ld_tok = [local(tokens.at[:, pl.ds(k * 1024, 1024)], tok.at[:, pl.ds(k * 1024, 1024)]) for k in range(8)]
    ld_s = local(sign, signv)
    ld_sc = local(scale, scalev)
    ld_f = [local(s, fl.at[k]) for k, s in enumerate((ll, gl, ml, pend_l))]
    ld_f += [local(s, fr.at[k]) for k, s in enumerate((lr, gr, mr, pend_r))]

    ld_w.wait()
    both_bits = lax.broadcasted_iota(jnp.int32, (256, 256), 0) & lax.broadcasted_iota(jnp.int32, (256, 256), 1)
    for b in (4, 2, 1):
        both_bits = both_bits ^ (both_bits >> b)
    had = (1 - 2 * (both_bits & 1)).astype(F32).astype(BF)
    w1 = (nn(had, wsh[...]) * (1.0 / math.sqrt(8192))).astype(BF)
    wg[c, 0, xl, y, z] = w1[:128]
    wg[c, 1, xl, z, y] = w1[128:]
    pl.semaphore_wait(barrier, len(peers))

    pos = [(y, z), (z, y)]

    def out_dev(q, d):
        return dev(dy=d) if q == 0 else dev(dz=d)

    def in_dev(q, d):
        return dev(dz=d) if q == 0 else dev(dy=d)

    w_in, w_po, w_pf, w_px, w_sib = ([{}, {}] for _ in range(5))

    def wp(q, do, di):
        o, i = pos[q]
        return wg.at[c, q, xl, mod4(o + do), mod4(i + di)]

    def x_dev(q):
        return dev(dx=-1 if q == 0 else 1)

    def w_out(q, di):
        ref = wp(q, 0, di)
        for d in (1, -1):
            w_po[q][di, d] = push(ref, ref, out_dev(q, d))

    def w_cross(q, do, di):
        ref = wp(q, do, di)
        w_px[q][do, di] = push(ref, ref, x_dev(q))

    def w_share(q, far, do):
        ref = wg.at[c, q, xl1 if far else xl, mod4(pos[q][0] + do)]
        w_sib[q][far, do] = push(ref, ref, dev(dc=1))

    def w_1(q):
        ref = wp(q, 0, 0)
        for d in (1, -1):
            w_in[q][d] = push(ref, ref, in_dev(q, d))
        w_out(q, 0)
        w_cross(q, 0, 0)

    def w_2(q):
        for d, h in ((1, 0), (-1, 64)):
            w_in[q][d].wait_recv()
            o, i = pos[q]
            ref = wg.at[c, q, xl, o, mod4(i - d), pl.ds(h, 64)]
            w_in[q][2 * d] = push(ref, ref, in_dev(q, d))
            w_out(q, -d)
            w_cross(q, 0, -d)

    def w_fwd(q, d, di):
        ref = wp(q, -d, di)
        w_pf[q][di] = push(ref, ref, out_dev(q, d))

    def w_got(q, d, di):
        w_po[q][di, d].wait_recv()
        w_cross(q, -d, di)
        if (d == 1) == (di in (0, 1)):
            w_fwd(q, d, di)

    def w_3(q):
        for d in (1, -1):
            w_got(q, d, 0)
        for d in (1, -1):
            w_in[q][2 * d].wait_recv()
        w_out(q, 2)
        w_cross(q, 0, 2)
        w_share(q, 0, 0)

    def w_4(q):
        for di in (1, -1):
            for d in (1, -1):
                w_got(q, d, di)

    def w_5(q):
        for d in (1, -1):
            w_got(q, d, 2)
            w_share(q, 0, -d)

    def w_6(q):
        for di in (0, 1, -1, 2):
            w_pf[q][di].wait_recv()
            w_cross(q, 2, di)
        w_share(q, 0, 2)

    def w_7(q, do):
        for di in (0, 1, -1, 2):
            w_px[q][do, di].wait_recv()
        w_share(q, 1, do)

    a_x, a_i, a_o = {}, [{}, {}], [{}, {}]

    def apiece(q, i, xs=slice(None)):
        return ag.at[y, i, xs, 0] if q == 0 else ag.at[i, z, xs, 1]

    def agrp(q, o, i=slice(None)):
        return ag.at[o, i, :, 0] if q == 0 else ag.at[i, o, :, 1]

    def a_x1():
        a_x[0] = push(a_in, ag.at[y, z, xl], xpair())

    def a_in1(q):
        if q == 0:
            ld_a.wait()
            a_x[0].wait_recv()
        ref = apiece(q, pos[q][1])
        for d in (1, -1):
            a_i[q][d] = push(ref, ref, in_dev(q, d))

    def a_in2(q):
        for d, h in ((1, 0), (-1, 1)):
            a_i[q][d].wait_recv()
            ref = apiece(q, mod4(pos[q][1] - d), h)
            a_i[q][2 * d] = push(ref, ref, in_dev(q, d))

    def a_out1(q):
        for d in (1, -1):
            a_i[q][2 * d].wait_recv()
        ref = agrp(q, pos[q][0])
        for d in (1, -1):
            a_o[q][d] = push(ref, ref, out_dev(q, d))

    def a_out2(q):
        for d, h in ((1, 0), (-1, 2)):
            a_o[q][d].wait_recv()
            ref = agrp(q, mod4(pos[q][0] - d), pl.ds(h, 2))
            a_o[q][2 * d] = push(ref, ref, out_dev(q, d))

    def a_out3(q):
        for d in (1, -1):
            a_o[q][2 * d].wait_recv()

    rs = {}

    def gat(q, t, o, i, xs):
        return (o, i, xs, 2 * q + t) if q == 0 else (i, o, xs, 2 * q + t)

    def gref(q, t, o, i, xs=slice(None)):
        return g.at[gat(q, t, o, i, xs)]

    def add_to(q, t, o, i, xv, *terms):
        at = gat(q, t, o, i, xv)
        total = g[at].astype(F32)
        for v in terms:
            total = total + v.astype(F32)
        g[at] = total.astype(BF)

    def rs_1(q, t):
        o = mod4(pos[q][0] + 2)
        for k, (d, h) in enumerate(((1, 0), (-1, 2))):
            rs[q, t, 1, d] = push(gref(q, t, o, pl.ds(h, 2)), r1.at[2 * q + t, k], out_dev(q, d))

    def rs_2(q, t):
        for k, (d, h) in enumerate(((1, 0), (-1, 2))):
            rs[q, t, 1, d].wait_recv()
            o = mod4(pos[q][0] + d)
            for j in range(4):
                add_to(q, t, o, h + j // 2, j % 2, r1[2 * q + t, k, j // 2, j % 2])
            rs[q, t, 2, d] = push(gref(q, t, o, slice(None)), r2.at[2 * q + t, k], out_dev(q, d))

    def rs_sum(q, t, di):
        p, i = 2 * q + t, mod4(pos[q][1] + di)
        for k in range(2):
            add_to(q, t, pos[q][0], i, k, r2[p, 0, i, k], r2[p, 1, i, k])

    def rs_3(q, t):
        o, i = pos[q][0], mod4(pos[q][1] + 2)
        for d in (1, -1):
            rs[q, t, 2, d].wait_recv()
        rs_sum(q, t, 2)
        for k, d in enumerate((1, -1)):
            rs[q, t, 4, d] = push(gref(q, t, o, i, k), r3.at[2 * q + t, k], in_dev(q, d))
        for di in (1, -1, 0):
            rs_sum(q, t, di)

    def rs_5(q, t):
        o = pos[q][0]
        for k, d in enumerate((1, -1)):
            rs[q, t, 4, d].wait_recv()
            i = mod4(pos[q][1] + d)
            add_to(q, t, o, i, k, r3[2 * q + t, k])
            rs[q, t, 5, d] = push(gref(q, t, o, i), r4.at[2 * q + t, k], in_dev(q, d))

    def rs_6(q, t):
        o, i = pos[q]
        for d in (1, -1):
            rs[q, t, 5, d].wait_recv()
        add_to(q, t, o, i, xl1, r4[2 * q + t, 0, xl1], r4[2 * q + t, 1, xl1])
        rs[q, t, 6] = push(gref(q, t, o, i, xl1), r5.at[2 * q + t], xpair())
        add_to(q, t, o, i, xl, r4[2 * q + t, 0, xl], r4[2 * q + t, 1, xl])

    def rs_7(t):
        for q in range(2):
            rs[q, t, 6].wait_recv()
            total = g[gat(q, t, *pos[q], xl)].astype(F32) + r5[2 * q + t].astype(F32)
            gin_t[(2 * q + t) * 64 : (2 * q + t) * 64 + 64] = total * shrink

    def back():
        ld_up.wait()
        ld_cot.wait()
        for k in range(3):
            bt[:, k * 256 : (k + 1) * 256] = (nt(upv[...], cotv[k * 256 : (k + 1) * 256, :]) * ADAPTER_SCALE).astype(BF)

    def grad_in(ks):
        for k in ks:
            ld_tok[k].wait()

        def one(j, carry):
            cols = pl.ds(pl.multiple_of(j * 1024, 1024), 1024)
            part = nn(bt[...], tok[:, cols]).astype(BF)
            for n in range(4):
                for p in range(4):
                    g[j // 2, (j % 2) * 2 + n // 2, n % 2, p] = part[p * 64 : p * 64 + 64, n * 256 : n * 256 + 256]
            return carry

        lax.fori_loop(ks[0], ks[-1] + 1, one, 0)

    def signs():
        ld_s.wait()

        def one(k, carry):
            cols = pl.ds(pl.multiple_of(k * 1024, 1024), 1024)
            flip = (1 - 2 * signv[:, cols]).astype(F32)
            sgn[:, cols] = jnp.broadcast_to(flip, (16, 1024)).astype(BF)
            return carry

        lax.fori_loop(0, 8, one, 0)

    def rotate(lo, hi):
        def one(k, carry):
            rows = pl.ds(pl.multiple_of(k * 16, 16), 16)
            st[...] = tok[rows] * sgn[...]
            for q in range(2):
                parts = [st[:, j * 256 + q * 128 : j * 256 + q * 128 + 128] for j in range(32)]
                for b in range(5):
                    step = 1 << b
                    for j in range(32):
                        if not j & step:
                            u, v = parts[j], parts[j + step]
                            parts[j], parts[j + step] = u + v, u - v
                for j in range(32):
                    jy, jz, jx = j // 8, (j // 2) % 4, j % 2
                    t = q * 32 + jx * 16 + (1 - q) * (jy * 4 + jz) + q * (jz * 4 + jy)
                    tok[rows, t * 128 : t * 128 + 128] = parts[j]
            return carry

        lax.fori_loop(lo, hi, one, 0)

    def frozen(q, xv, d, ch, first=False):
        o = mod4(pos[q][0] + d)
        at = pl.multiple_of(((q * 2 + xv) * 4 + o) * 512, 512)
        part = nn(tok[:, pl.ds(at, 512)], wg[ch, q, xv, o].reshape(512, 512))
        if first:
            acc[ch] = part
        else:
            acc[ch] += part

    def low_start():
        for cp in col_copies(0) + col_copies(1):
            cp.start()

    def low_rank(lo, hi):
        def one(k, carry):
            for cp in col_copies(k):
                cp.wait()
            cy, cz = low_chunk(k)
            part = nn(sl[k % 2], ag[cy, pl.ds(cz * 2, 2)].reshape(1024, 256))
            low[...] = jnp.where(k == 0, part, low[...] + part)

            @pl.when(k + 2 < 8)
            def _():
                for cp in col_copies(k + 2):
                    cp.start()

            return carry

        lax.fori_loop(lo, hi, one, 0)

    fx = {}

    def frag_1():
        for cp in ld_f:
            cp.wait()
        for buf, d in ((fl, dl), (fr, dr)):
            n = buf.shape[1]
            for h in range(2):
                rows = slice(h * n // 2, (h + 1) * n // 2)
                lv, gv, mv, pv = (buf[k, rows] for k in range(4))
                nm = MOMENTUM * mv + pv
                buf[2, rows] = nm
                buf[0, rows] = gv - OUTER_RATE * (pv + MOMENTUM * nm)
                d[h] = (gv - lv).astype(BF)
        fx["l"] = push(dl.at[c1], dl1, dev(dc=1))
        fx["r"] = push(dr.at[c1], dr1, dev(dc=1))
        return [local(fl.at[0], o_gl), local(fr.at[0], o_gr), local(fl.at[2], o_ml), local(fr.at[2], o_mr)]

    def frag_2():
        for k, d, d1, d2 in (("l", dl, dl1, dl2), ("r", dr, dr1, dr2)):
            fx[k].wait_recv()
            d1[...] = (d1[...].astype(F32) + d[c].astype(F32)).astype(BF)
            fx[k + "x"] = push(d1, d2, dev(dx=2))

    def frag_3():
        for k, d1, d2, buf in (("l", dl1, dl2, fl), ("r", dr1, dr2, fr)):
            fx[k + "x"].wait_recv()
            n = buf.shape[1] // 2
            rows = pl.ds(pl.multiple_of(c * n, n), n)
            buf[3, rows] = (d1[...].astype(F32) + d2[...].astype(F32)) * 0.25
            fx[k + "s"] = push(buf.at[3, rows], buf.at[3, rows], dev(dc=1))

    def frag_4():
        for k in "lr":
            fx[k + "s"].wait_recv()
        return [local(fl.at[3], o_pl), local(fr.at[3], o_pr)]

    gx = {}

    def gout_1():
        lt = low[...].T.astype(BF)
        for q in range(2):
            part = nn(lt, cotv[:, q * 512 : (q + 1) * 512]) * (ADAPTER_SCALE * shrink)
            go[q] = part.astype(BF).reshape(4, 4, 16, 512)
        for q in range(2):
            for k, d in enumerate((1, -1, 2)):
                o = mod4(pos[q][0] + d)
                src = go.at[0, o] if q == 0 else go.at[1, :, o]
                gx[q, 1, k] = push(src, go_o.at[q, k], out_dev(q, d))

    def gout_2():
        for q in range(2):
            for k in range(3):
                gx[q, 1, k].wait_recv()
            own = go[0, y] if q == 0 else go[1, :, z]
            total = own.astype(F32)
            for k in range(3):
                total = total + go_o[q, k].astype(F32)
            go_f[q] = total

    def gout_2s():
        for q in range(2):
            for k, d in enumerate((1, -1, 2)):
                i = mod4(pos[q][1] + d)
                gx[q, 2, k] = push(go_f.at[q, i], go_i.at[q, k], in_dev(q, d))

    def gout_3():
        for q in range(2):
            for k in range(3):
                gx[q, 2, k].wait_recv()
            total = go_f[q, pos[q][1]]
            for k in range(3):
                total = total + go_i[q, k]
            go_x[:, :, q * 512 : (q + 1) * 512] = total.reshape(2, 8, 512)
        gx["x"] = push(go_x.at[xl1], gout.at[1], xpair())

    def gout_4():
        gx["x"].wait_recv()
        gout[0] = go_x[xl] + gout[1]
        return [local(gout.at[0], o_gout)]

    outs = []

    def column_sums(ch):
        cols = slice(ch * 512, (ch + 1) * 512)
        sums = jnp.zeros((1, 512), F32)
        for k in range(3):
            rows = slice(k * 256, (k + 1) * 256)
            sums = sums + jnp.sum(cotv[rows, cols].astype(F32) * acc[ch, rows], axis=0, keepdims=True)
        gs[0:1, cols] = sums * shrink

    def mixture(ch):
        cols = slice(ch * 512, (ch + 1) * 512)
        lowb = low[...].astype(BF)
        for k in range(3):
            rows = slice(k * 256, (k + 1) * 256)
            mix = acc[ch, rows] * scalev[:, cols] + ADAPTER_SCALE * nn(lowb[rows], upv[:, cols])
            val[rows, cols] = mix.astype(BF)

    sx = {}

    def scale_x():
        sx["x"] = push(gs.at[0:1], gs_o.at[6:7], xpair())

    def scale_i():
        sx["x"].wait_recv()
        gs[1:2] = gs[0:1] + gs_o[6:7]
        for k, d in enumerate((1, -1, 2)):
            sx["i", k] = push(gs.at[1:2], gs_o.at[k : k + 1], dev(dz=d))

    def scale_o():
        for k in range(3):
            sx["i", k].wait_recv()
        gs[2:3] = (gs[1:2] + gs_o[2:3]) + (gs_o[0:1] + gs_o[1:2])
        for k, d in enumerate((1, -1, 2)):
            sx["o", k] = push(gs.at[2:3], gs_o.at[3 + k : 4 + k], dev(dy=d))

    def scale_f():
        for k in range(3):
            sx["o", k].wait_recv()
        gs[3:4] = (gs[2:3] + gs_o[5:6]) + (gs_o[3:4] + gs_o[4:5])
        return [local(gs.at[3:4], o_gs)]

    def both(fn, *args):
        fn(0, *args)
        fn(1, *args)

    def drain(keep):
        while len(sent) > keep:
            sent.pop(0).wait_send()

    def use(far, do):
        for q in range(2):
            w_sib[q][far, do].wait_recv()
            for ch in range(2):
                frozen(q, xl1 if far else xl, do, ch, first=far == 0 and do == 0 and q == 0)

    both(w_1)
    a_x1()
    back()
    grad_in([0, 1])
    both(w_2)
    grad_in([2, 3, 4, 5])
    both(a_in1)
    both(w_3)
    grad_in([6, 7])
    signs()
    rotate(0, 24)
    both(w_4)
    both(a_in2)
    rotate(24, 48)
    both(w_5)
    both(a_out1)
    low_start()
    outs += frag_1()
    use(0, 0)
    both(w_6)
    use(0, 1)
    use(0, -1)
    frag_2()
    both(a_out2)
    both(rs_1, 0)
    both(rs_1, 1)
    low_rank(0, 3)
    for q in range(2):
        w_7(q, 0)
    use(0, 2)
    use(1, 0)
    for do in (1, -1):
        for q in range(2):
            w_7(q, do)
    both(a_out3)
    both(rs_2, 0)
    both(rs_2, 1)
    low_rank(3, 8)
    gout_1()
    use(1, 1)
    use(1, -1)
    for q in range(2):
        w_7(q, 2)
    frag_3()
    use(1, 2)
    for ch in range(2):
        column_sums(ch)
    scale_x()
    both(rs_3, 0)
    both(rs_3, 1)
    ld_sc.wait()
    mixture(0)
    gout_2()
    gout_2s()
    both(rs_5, 0)
    both(rs_5, 1)
    scale_i()
    mixture(1)
    outs.append(local(val, o_val))
    outs += frag_4()
    drain(24)
    gout_3()
    both(rs_6, 0)
    both(rs_6, 1)
    scale_o()
    outs += gout_4()
    drain(7)
    rs_7(0)
    rs_7(1)
    gin[...] = gin_t[...].T
    outs.append(local(gin, o_gin))
    outs += scale_f()
    for cp in sent:
        cp.wait_send()
    for cp in outs:
        cp.wait()


def call(*args):
    vm = pltpu.VMEM
    out = [
        jax.ShapeDtypeStruct((ROWS, 1024), BF),
        jax.ShapeDtypeStruct((256, 256), F32),
        jax.ShapeDtypeStruct((8, 1024), F32),
        jax.ShapeDtypeStruct((1, 1024), F32),
        jax.ShapeDtypeStruct((1024, 256), F32),
        jax.ShapeDtypeStruct((32, 1024), F32),
        jax.ShapeDtypeStruct((1024, 256), F32),
        jax.ShapeDtypeStruct((32, 1024), F32),
        jax.ShapeDtypeStruct((1024, 256), F32),
        jax.ShapeDtypeStruct((32, 1024), F32),
    ]
    scratch = [
        vm((2, 2, 2, 4, 4, 128, 512), BF),
        vm((4, 4, 2, 2, 128, 256), BF),
        vm((ROWS, 8192), BF),
        vm((16, 8192), BF),
        vm((16, 8192), BF),
        vm((2, ROWS, 1024), BF),
        vm((4, 4, 2, 4, 64, 256), BF),
        vm((4, 2, 2, 2, 64, 256), BF),
        vm((4, 2, 4, 2, 64, 256), BF),
        vm((4, 2, 64, 256), BF),
        vm((4, 2, 2, 64, 256), BF),
        vm((4, 64, 256), BF),
        vm((ROWS, 1024), BF),
        vm((256, 1024), BF),
        vm((2, ROWS, 512), F32),
        vm((ROWS, 256), F32),
        vm((256, ROWS), BF),
        vm((ROWS, 1024), BF),
        vm((1, 8192), jnp.int32),
        vm((1, 1024), F32),
        vm((256, 512), BF),
        vm((2, 4, 4, 16, 512), BF),
        vm((2, 3, 4, 16, 512), BF),
        vm((2, 3, 16, 512), F32),
        vm((2, 8, 1024), F32),
        vm((2, 4, 16, 512), F32),
        vm((8, 1024), F32),
        vm((8, 1024), F32),
        vm((4, 1024, 256), F32),
        vm((4, 32, 1024), F32),
        vm((2, 512, 256), BF),
        vm((2, 16, 1024), BF),
        vm((512, 256), BF),
        vm((16, 1024), BF),
        vm((512, 256), BF),
        vm((16, 1024), BF),
        vm((256, 256), F32),
        vm((256, 256), F32),
        vm((2, 8, 1024), F32),
        pltpu.SemaphoreType.DMA((NSEM,)),
        pltpu.SemaphoreType.DMA((NSEM,)),
        pltpu.SemaphoreType.DMA((40,)),
        pltpu.SemaphoreType.DMA((2, 4)),
    ]
    hbm = pl.BlockSpec(memory_space=pl.ANY)
    return pl.pallas_call(
        body,
        name="step",
        out_shape=out,
        in_specs=[hbm] * len(args),
        out_specs=[hbm] * len(out),
        scratch_shapes=scratch,
        compiler_params=pltpu.CompilerParams(
            collective_id=0, has_side_effects=True, vmem_limit_bytes=64 * 1024 * 1024
        ),
        cost_estimate=pl.CostEstimate(flops=23_000_000_000, bytes_accessed=30_000_000, transcendentals=0),
    )(*args)


def hand_over(refs):
    n = len(refs)
    parts = []
    for k, a in enumerate(refs):
        parts.append((k, pl.ds(0, a.shape[0])))

    def copy_all(*args):
        src, dst, held = args[:n], args[n : 2 * n], args[2 * n : 3 * n]
        sem_in, sem_out = args[3 * n :]
        into, away = [], []
        for m, (k, rows) in enumerate(parts):
            into.append(pltpu.make_async_copy(src[k].at[rows], held[k].at[rows], sem_in.at[m]))
            away.append(pltpu.make_async_copy(held[k].at[rows], dst[k].at[rows], sem_out.at[m]))
        for cp in into:
            cp.start()
        for a, b in zip(into, away):
            a.wait()
            b.start()
        for cp in away:
            cp.wait()

    hbm = pl.BlockSpec(memory_space=pl.ANY)
    return pl.pallas_call(
        copy_all,
        name="hand_over",
        out_shape=[jax.ShapeDtypeStruct(a.shape, a.dtype) for a in refs],
        in_specs=[hbm] * n,
        out_specs=[hbm] * n,
        scratch_shapes=[pltpu.VMEM(a.shape, a.dtype) for a in refs]
        + [pltpu.SemaphoreType.DMA((len(parts),))] * 2,
        compiler_params=pltpu.CompilerParams(vmem_limit_bytes=60 * 1024 * 1024),
    )(*refs)


def per_device(
    tokens, sign_bits, base_weight, learned_column_scale, adapter_in, adapter_up_weight, out_cotangent,
    local_left, local_right, global_left, global_right, moment_left, moment_right, pending_left, pending_right,
):
    left = [a.reshape(1024, 256) for a in (local_left, global_left, moment_left, pending_left)]
    right = [a.reshape(32, 1024) for a in (local_right, global_right, moment_right, pending_right)]
    pairs = [a for pair in zip(left, right) for a in pair]
    out = call(
        tokens, sign_bits.reshape(1, 8192), base_weight, learned_column_scale.reshape(1, 1024),
        adapter_in.reshape(2, 128, 256), adapter_up_weight.reshape(256, 1024), out_cotangent, *pairs,
    )
    val, gin, gout, gs, gl, gr, ml, mr, pdl, pdr = out
    return hand_over((
        val, gin[None], gout[None], gs,
        gl.reshape(4, 256, 256), gr.reshape(4, 8, 1024), ml.reshape(4, 256, 256), mr.reshape(4, 8, 1024),
        pdl.reshape(4, 256, 256), pdr.reshape(4, 8, 1024),
    ))


def solution(mesh):
    rows, frag = P(("replica", "fsdp"), None), P(None, "fsdp", None)
    return jax.shard_map(
        per_device,
        mesh=mesh,
        in_specs=(
            rows, P(), P("fsdp", None), P(), P("replica", "fsdp", None), P("replica", None, None), rows,
            P("replica", None, "fsdp", None), P("replica", None, "fsdp", None),
        ) + (frag,) * 6,
        out_specs=(rows, P("replica", "fsdp", None), P("replica", "fsdp", None), P("replica", None)) + (frag,) * 6,
        check_vma=False,
    )
```

```python
import math

import jax
import jax.numpy as jnp
from jax import lax
from jax.experimental import pallas as pl
from jax.experimental.pallas import tpu as pltpu
from jax.sharding import PartitionSpec as P

MESH = pl.DeviceIdType.MESH
BF = jnp.bfloat16
F32 = jnp.float32
ADAPTER_SCALE = 2.0
MOMENTUM = 0.9
OUTER_RATE = 0.7
ROWS = 768
NSEM = 224


def nt(a, b):
    return lax.dot_general(a, b, (((1,), (1,)), ((), ())), preferred_element_type=F32)


def nn(a, b):
    return jnp.dot(a, b, preferred_element_type=F32)


def body(
    tokens, sign, weight, scale, a_in, up, cot, ll, lr, gl, gr, ml, mr, pend_l, pend_r,
    o_val, o_gin, o_gout, o_gs, o_gl, o_gr, o_ml, o_mr, o_pl, o_pr,
    wg, ag, tok, st, sgn, sl, g, r1, r2, r3, r4, r5, cotv, upv, acc, low, bt, val, signv, scalev, wsh,
    go, go_o, go_i, go_x, go_f, gs, gs_o, fl, fr, dl, dr, dl1, dr1, dl2, dr2, gin_t, gin, gout,
    send, recv, loc, sl_sem,
):
    r, f = lax.axis_index("replica"), lax.axis_index("fsdp")
    xh, c = r // 2, r % 2
    y, z, xl = f // 8, (f // 2) % 4, f % 2
    c1, xl1 = 1 - c, 1 - xl
    shrink = 1.0 / math.sqrt(ROWS * 32)

    def dev(dx=0, dy=0, dz=0, dc=0):
        x = (2 * xh + xl + dx + 4) % 4
        return ((x // 2) * 2 + (c + dc) % 2, ((y + dy + 4) % 4) * 8 + ((z + dz + 4) % 4) * 2 + x % 2)

    def xpair():
        return (r, y * 8 + z * 2 + xl1)

    def mod4(v):
        return (v + 4) % 4

    barrier = pltpu.get_barrier_semaphore()
    peers = [dev(dx=1), dev(dx=-1), dev(dx=2), dev(dy=1), dev(dy=-1), dev(dy=2), dev(dz=1), dev(dz=-1), dev(dz=2), dev(dc=1)]
    for p in peers:
        pl.semaphore_signal(barrier, inc=1, device_id=p, device_id_type=MESH)

    nloc = [0]

    def local(src, dst):
        cp = pltpu.make_async_copy(src, dst, loc.at[nloc[0]])
        nloc[0] += 1
        cp.start()
        return cp

    nrem = [0]
    sent = []

    def push(src, dst, where):
        k = nrem[0]
        nrem[0] += 1
        cp = pltpu.make_async_remote_copy(
            src_ref=src, dst_ref=dst, send_sem=send.at[k], recv_sem=recv.at[k],
            device_id=where, device_id_type=MESH,
        )
        cp.start()
        sent.append(cp)
        return cp

    def low_chunk(k):
        n = k % 4
        return mod4(y + (n ^ (n // 2))), (z // 2 + k // 4) % 2

    def col_copies(k):
        cy, cz = low_chunk(k)
        cols = pl.ds(pl.multiple_of(cy * 2048 + cz * 1024, 1024), 1024)
        return [
            pltpu.make_async_copy(
                tokens.at[pl.ds(n * 192, 192), cols], sl.at[k % 2, pl.ds(n * 192, 192)], sl_sem.at[k % 2, n]
            )
            for n in range(4)
        ]

    ld_w = local(weight.at[:, pl.ds(pl.multiple_of(c * 512, 512), 512)], wsh)
    ld_up = local(up, upv)
    ld_a = local(a_in, ag.at[y, z, xl])
    ld_cot = local(cot, cotv)
    ld_tok = [local(tokens.at[:, pl.ds(k * 1024, 1024)], tok.at[:, pl.ds(k * 1024, 1024)]) for k in range(8)]
    ld_s = local(sign, signv)
    ld_sc = local(scale, scalev)
    ld_f = [local(s, fl.at[k]) for k, s in enumerate((ll, gl, ml, pend_l))]
    ld_f += [local(s, fr.at[k]) for k, s in enumerate((lr, gr, mr, pend_r))]

    ld_w.wait()
    both_bits = lax.broadcasted_iota(jnp.int32, (256, 256), 0) & lax.broadcasted_iota(jnp.int32, (256, 256), 1)
    for b in (4, 2, 1):
        both_bits = both_bits ^ (both_bits >> b)
    had = (1 - 2 * (both_bits & 1)).astype(F32).astype(BF)
    w1 = (nn(had, wsh[...]) * (1.0 / math.sqrt(8192))).astype(BF)
    wg[c, 0, xl, y, z] = w1[:128]
    wg[c, 1, xl, z, y] = w1[128:]
    pl.semaphore_wait(barrier, len(peers))

    pos = [(y, z), (z, y)]

    def out_dev(q, d):
        return dev(dy=d) if q == 0 else dev(dz=d)

    def in_dev(q, d):
        return dev(dz=d) if q == 0 else dev(dy=d)

    w_in, w_po, w_pf, w_px, w_sib = ([{}, {}] for _ in range(5))

    def wp(q, do, di):
        o, i = pos[q]
        return wg.at[c, q, xl, mod4(o + do), mod4(i + di)]

    def x_dev(q):
        return dev(dx=-1 if q == 0 else 1)

    def w_out(q, di):
        ref = wp(q, 0, di)
        for d in (1, -1):
            w_po[q][di, d] = push(ref, ref, out_dev(q, d))

    def w_cross(q, do, di):
        ref = wp(q, do, di)
        w_px[q][do, di] = push(ref, ref, x_dev(q))

    def w_share(q, far, do):
        ref = wg.at[c, q, xl1 if far else xl, mod4(pos[q][0] + do)]
        w_sib[q][far, do] = push(ref, ref, dev(dc=1))

    def w_1(q):
        ref = wp(q, 0, 0)
        for d in (1, -1):
            w_in[q][d] = push(ref, ref, in_dev(q, d))
        w_out(q, 0)
        w_cross(q, 0, 0)

    def w_2(q):
        for d, h in ((1, 0), (-1, 64)):
            w_in[q][d].wait_recv()
            o, i = pos[q]
            ref = wg.at[c, q, xl, o, mod4(i - d), pl.ds(h, 64)]
            w_in[q][2 * d] = push(ref, ref, in_dev(q, d))
            w_out(q, -d)
            w_cross(q, 0, -d)

    def w_fwd(q, d, di):
        ref = wp(q, -d, di)
        w_pf[q][di] = push(ref, ref, out_dev(q, d))

    def w_got(q, d, di):
        w_po[q][di, d].wait_recv()
        w_cross(q, -d, di)
        if (d == 1) == (di in (0, 1)):
            w_fwd(q, d, di)

    def w_3(q):
        for d in (1, -1):
            w_got(q, d, 0)
        for d in (1, -1):
            w_in[q][2 * d].wait_recv()
        w_out(q, 2)
        w_cross(q, 0, 2)
        w_share(q, 0, 0)

    def w_4(q):
        for di in (1, -1):
            for d in (1, -1):
                w_got(q, d, di)

    def w_5(q):
        for d in (1, -1):
            w_got(q, d, 2)
            w_share(q, 0, -d)

    def w_6(q):
        for di in (0, 1, -1, 2):
            w_pf[q][di].wait_recv()
            w_cross(q, 2, di)
        w_share(q, 0, 2)

    def w_7(q, do):
        for di in (0, 1, -1, 2):
            w_px[q][do, di].wait_recv()
        w_share(q, 1, do)

    a_x, a_i, a_o = {}, [{}, {}], [{}, {}]

    def apiece(q, i, xs=slice(None)):
        return ag.at[y, i, xs, 0] if q == 0 else ag.at[i, z, xs, 1]

    def agrp(q, o, i=slice(None)):
        return ag.at[o, i, :, 0] if q == 0 else ag.at[i, o, :, 1]

    def a_x1():
        a_x[0] = push(a_in, ag.at[y, z, xl], xpair())

    def a_in1(q):
        if q == 0:
            ld_a.wait()
            a_x[0].wait_recv()
        ref = apiece(q, pos[q][1])
        for d in (1, -1):
            a_i[q][d] = push(ref, ref, in_dev(q, d))

    def a_in2(q):
        for d, h in ((1, 0), (-1, 1)):
            a_i[q][d].wait_recv()
            ref = apiece(q, mod4(pos[q][1] - d), h)
            a_i[q][2 * d] = push(ref, ref, in_dev(q, d))

    def a_out1(q):
        for d in (1, -1):
            a_i[q][2 * d].wait_recv()
        ref = agrp(q, pos[q][0])
        for d in (1, -1):
            a_o[q][d] = push(ref, ref, out_dev(q, d))

    def a_out2(q):
        for d, h in ((1, 0), (-1, 2)):
            a_o[q][d].wait_recv()
            ref = agrp(q, mod4(pos[q][0] - d), pl.ds(h, 2))
            a_o[q][2 * d] = push(ref, ref, out_dev(q, d))

    def a_out3(q):
        for d in (1, -1):
            a_o[q][2 * d].wait_recv()

    rs = {}

    def gat(q, t, o, i, xs):
        return (o, i, xs, 2 * q + t) if q == 0 else (i, o, xs, 2 * q + t)

    def gref(q, t, o, i, xs=slice(None)):
        return g.at[gat(q, t, o, i, xs)]

    def add_to(q, t, o, i, xv, *terms):
        at = gat(q, t, o, i, xv)
        total = g[at].astype(F32)
        for v in terms:
            total = total + v.astype(F32)
        g[at] = total.astype(BF)

    def rs_1(q, t):
        o = mod4(pos[q][0] + 2)
        for k, (d, h) in enumerate(((1, 0), (-1, 2))):
            rs[q, t, 1, d] = push(gref(q, t, o, pl.ds(h, 2)), r1.at[2 * q + t, k], out_dev(q, d))

    def rs_2(q, t):
        for k, (d, h) in enumerate(((1, 0), (-1, 2))):
            rs[q, t, 1, d].wait_recv()
            o = mod4(pos[q][0] + d)
            for j in range(4):
                add_to(q, t, o, h + j // 2, j % 2, r1[2 * q + t, k, j // 2, j % 2])
            rs[q, t, 2, d] = push(gref(q, t, o, slice(None)), r2.at[2 * q + t, k], out_dev(q, d))

    def rs_sum(q, t, di):
        p, i = 2 * q + t, mod4(pos[q][1] + di)
        for k in range(2):
            add_to(q, t, pos[q][0], i, k, r2[p, 0, i, k], r2[p, 1, i, k])

    def rs_3(q, t):
        o, i = pos[q][0], mod4(pos[q][1] + 2)
        for d in (1, -1):
            rs[q, t, 2, d].wait_recv()
        rs_sum(q, t, 2)
        for k, d in enumerate((1, -1)):
            rs[q, t, 4, d] = push(gref(q, t, o, i, k), r3.at[2 * q + t, k], in_dev(q, d))

    def rs_4(q, t):
        for di in (1, -1, 0):
            rs_sum(q, t, di)

    def rs_5(q, t):
        o = pos[q][0]
        for k, d in enumerate((1, -1)):
            rs[q, t, 4, d].wait_recv()
            i = mod4(pos[q][1] + d)
            add_to(q, t, o, i, k, r3[2 * q + t, k])
            rs[q, t, 5, d] = push(gref(q, t, o, i), r4.at[2 * q + t, k], in_dev(q, d))

    def rs_6(q, t):
        o, i = pos[q]
        for d in (1, -1):
            rs[q, t, 5, d].wait_recv()
        add_to(q, t, o, i, xl1, r4[2 * q + t, 0, xl1], r4[2 * q + t, 1, xl1])
        rs[q, t, 6] = push(gref(q, t, o, i, xl1), r5.at[2 * q + t], xpair())
        add_to(q, t, o, i, xl, r4[2 * q + t, 0, xl], r4[2 * q + t, 1, xl])

    def rs_7(t):
        for q in range(2):
            rs[q, t, 6].wait_recv()
            total = g[gat(q, t, *pos[q], xl)].astype(F32) + r5[2 * q + t].astype(F32)
            gin_t[(2 * q + t) * 64 : (2 * q + t) * 64 + 64] = total * shrink

    def back():
        ld_up.wait()
        ld_cot.wait()
        for k in range(3):
            bt[:, k * 256 : (k + 1) * 256] = (nt(upv[...], cotv[k * 256 : (k + 1) * 256, :]) * ADAPTER_SCALE).astype(BF)

    def grad_in(ks):
        for k in ks:
            ld_tok[k].wait()

        def one(j, carry):
            cols = pl.ds(pl.multiple_of(j * 1024, 1024), 1024)
            part = nn(bt[...], tok[:, cols]).astype(BF)
            for n in range(4):
                for p in range(4):
                    g[j // 2, (j % 2) * 2 + n // 2, n % 2, p] = part[p * 64 : p * 64 + 64, n * 256 : n * 256 + 256]
            return carry

        lax.fori_loop(ks[0], ks[-1] + 1, one, 0)

    def signs():
        ld_s.wait()

        def one(k, carry):
            cols = pl.ds(pl.multiple_of(k * 1024, 1024), 1024)
            flip = (1 - 2 * signv[:, cols]).astype(F32)
            sgn[:, cols] = jnp.broadcast_to(flip, (16, 1024)).astype(BF)
            return carry

        lax.fori_loop(0, 8, one, 0)

    def rotate(lo, hi):
        def one(k, carry):
            rows = pl.ds(pl.multiple_of(k * 16, 16), 16)
            st[...] = tok[rows] * sgn[...]
            for q in range(2):
                parts = [st[:, j * 256 + q * 128 : j * 256 + q * 128 + 128] for j in range(32)]
                for b in range(5):
                    step = 1 << b
                    for j in range(32):
                        if not j & step:
                            u, v = parts[j], parts[j + step]
                            parts[j], parts[j + step] = u + v, u - v
                for j in range(32):
                    jy, jz, jx = j // 8, (j // 2) % 4, j % 2
                    t = q * 32 + jx * 16 + (1 - q) * (jy * 4 + jz) + q * (jz * 4 + jy)
                    tok[rows, t * 128 : t * 128 + 128] = parts[j]
            return carry

        lax.fori_loop(lo, hi, one, 0)

    def frozen(q, xv, d, ch, first=False):
        o = mod4(pos[q][0] + d)
        at = pl.multiple_of(((q * 2 + xv) * 4 + o) * 512, 512)
        part = nn(tok[:, pl.ds(at, 512)], wg[ch, q, xv, o].reshape(512, 512))
        if first:
            acc[ch] = part
        else:
            acc[ch] += part

    def low_start():
        for cp in col_copies(0) + col_copies(1):
            cp.start()

    def low_rank(lo, hi):
        def one(k, carry):
            for cp in col_copies(k):
                cp.wait()
            cy, cz = low_chunk(k)
            part = nn(sl[k % 2], ag[cy, pl.ds(cz * 2, 2)].reshape(1024, 256))
            low[...] = jnp.where(k == 0, part, low[...] + part)

            @pl.when(k + 2 < 8)
            def _():
                for cp in col_copies(k + 2):
                    cp.start()

            return carry

        lax.fori_loop(lo, hi, one, 0)

    fx = {}

    def frag_1():
        for cp in ld_f:
            cp.wait()
        for buf, d in ((fl, dl), (fr, dr)):
            n = buf.shape[1]
            for h in range(2):
                rows = slice(h * n // 2, (h + 1) * n // 2)
                lv, gv, mv, pv = (buf[k, rows] for k in range(4))
                nm = MOMENTUM * mv + pv
                buf[2, rows] = nm
                buf[0, rows] = gv - OUTER_RATE * (pv + MOMENTUM * nm)
                d[h] = (gv - lv).astype(BF)
        fx["l"] = push(dl.at[c1], dl1, dev(dc=1))
        fx["r"] = push(dr.at[c1], dr1, dev(dc=1))
        return [local(fl.at[0], o_gl), local(fr.at[0], o_gr), local(fl.at[2], o_ml), local(fr.at[2], o_mr)]

    def frag_2():
        for k, d, d1, d2 in (("l", dl, dl1, dl2), ("r", dr, dr1, dr2)):
            fx[k].wait_recv()
            d1[...] = (d1[...].astype(F32) + d[c].astype(F32)).astype(BF)
            fx[k + "x"] = push(d1, d2, dev(dx=2))

    def frag_3():
        for k, d1, d2, buf in (("l", dl1, dl2, fl), ("r", dr1, dr2, fr)):
            fx[k + "x"].wait_recv()
            n = buf.shape[1] // 2
            rows = pl.ds(pl.multiple_of(c * n, n), n)
            buf[3, rows] = (d1[...].astype(F32) + d2[...].astype(F32)) * 0.25
            fx[k + "s"] = push(buf.at[3, rows], buf.at[3, rows], dev(dc=1))

    def frag_4():
        for k in "lr":
            fx[k + "s"].wait_recv()
        return [local(fl.at[3], o_pl), local(fr.at[3], o_pr)]

    gx = {}

    def gout_1():
        lt = low[...].T.astype(BF)
        for q in range(2):
            part = nn(lt, cotv[:, q * 512 : (q + 1) * 512]) * (ADAPTER_SCALE * shrink)
            go[q] = part.astype(BF).reshape(4, 4, 16, 512)
        for q in range(2):
            for k, d in enumerate((1, -1, 2)):
                o = mod4(pos[q][0] + d)
                src = go.at[0, o] if q == 0 else go.at[1, :, o]
                gx[q, 1, k] = push(src, go_o.at[q, k], out_dev(q, d))

    def gout_2():
        for q in range(2):
            for k in range(3):
                gx[q, 1, k].wait_recv()
            own = go[0, y] if q == 0 else go[1, :, z]
            total = own.astype(F32)
            for k in range(3):
                total = total + go_o[q, k].astype(F32)
            go_f[q] = total

    def gout_2s():
        for q in range(2):
            for k, d in enumerate((1, -1, 2)):
                i = mod4(pos[q][1] + d)
                gx[q, 2, k] = push(go_f.at[q, i], go_i.at[q, k], in_dev(q, d))

    def gout_3():
        for q in range(2):
            for k in range(3):
                gx[q, 2, k].wait_recv()
            total = go_f[q, pos[q][1]]
            for k in range(3):
                total = total + go_i[q, k]
            go_x[:, :, q * 512 : (q + 1) * 512] = total.reshape(2, 8, 512)
        gx["x"] = push(go_x.at[xl1], gout.at[1], xpair())

    def gout_4():
        gx["x"].wait_recv()
        gout[0] = go_x[xl] + gout[1]
        return [local(gout.at[0], o_gout)]

    outs = []

    def column_sums(ch):
        cols = slice(ch * 512, (ch + 1) * 512)
        sums = jnp.zeros((1, 512), F32)
        for k in range(3):
            rows = slice(k * 256, (k + 1) * 256)
            sums = sums + jnp.sum(cotv[rows, cols].astype(F32) * acc[ch, rows], axis=0, keepdims=True)
        gs[0:1, cols] = sums * shrink

    def mixture(ch):
        cols = slice(ch * 512, (ch + 1) * 512)
        lowb = low[...].astype(BF)
        for k in range(3):
            rows = slice(k * 256, (k + 1) * 256)
            mix = acc[ch, rows] * scalev[:, cols] + ADAPTER_SCALE * nn(lowb[rows], upv[:, cols])
            val[rows, cols] = mix.astype(BF)

    sx = {}

    def scale_x():
        sx["x"] = push(gs.at[0:1], gs_o.at[6:7], xpair())

    def scale_i():
        sx["x"].wait_recv()
        gs[1:2] = gs[0:1] + gs_o[6:7]
        for k, d in enumerate((1, -1, 2)):
            sx["i", k] = push(gs.at[1:2], gs_o.at[k : k + 1], dev(dz=d))

    def scale_o():
        for k in range(3):
            sx["i", k].wait_recv()
        gs[2:3] = (gs[1:2] + gs_o[2:3]) + (gs_o[0:1] + gs_o[1:2])
        for k, d in enumerate((1, -1, 2)):
            sx["o", k] = push(gs.at[2:3], gs_o.at[3 + k : 4 + k], dev(dy=d))

    def scale_f():
        for k in range(3):
            sx["o", k].wait_recv()
        gs[3:4] = (gs[2:3] + gs_o[5:6]) + (gs_o[3:4] + gs_o[4:5])
        return [local(gs.at[3:4], o_gs)]

    def both(fn, *args):
        fn(0, *args)
        fn(1, *args)

    def drain(keep):
        while len(sent) > keep:
            sent.pop(0).wait_send()

    def use(far, do):
        for q in range(2):
            w_sib[q][far, do].wait_recv()
            for ch in range(2):
                frozen(q, xl1 if far else xl, do, ch, first=far == 0 and do == 0 and q == 0)

    both(w_1)
    a_x1()
    back()
    grad_in([0, 1])
    both(w_2)
    grad_in([2, 3, 4, 5])
    both(a_in1)
    both(w_3)
    grad_in([6, 7])
    signs()
    rotate(0, 24)
    both(w_4)
    both(a_in2)
    rotate(24, 48)
    both(w_5)
    both(a_out1)
    low_start()
    outs += frag_1()
    use(0, 0)
    both(w_6)
    use(0, 1)
    use(0, -1)
    both(a_out2)
    both(rs_1, 0)
    both(rs_1, 1)
    low_rank(0, 3)
    for q in range(2):
        w_7(q, 0)
    use(0, 2)
    use(1, 0)
    for do in (1, -1):
        for q in range(2):
            w_7(q, do)
    use(1, 1)
    both(a_out3)
    both(rs_2, 0)
    both(rs_2, 1)
    use(1, -1)
    low_rank(3, 8)
    gout_1()
    for q in range(2):
        w_7(q, 2)
    frag_2()
    use(1, 2)
    for ch in range(2):
        column_sums(ch)
    scale_x()
    ld_sc.wait()
    mixture(0)
    both(rs_3, 0)
    both(rs_3, 1)
    scale_i()
    both(rs_4, 0)
    both(rs_4, 1)
    gout_2()
    gout_2s()
    frag_3()
    both(rs_5, 0)
    both(rs_5, 1)
    mixture(1)
    outs.append(local(val, o_val))
    scale_o()
    both(rs_6, 0)
    both(rs_6, 1)
    gout_3()
    drain(24)
    outs += scale_f()
    outs += frag_4()
    rs_7(0)
    rs_7(1)
    gin[...] = gin_t[...].T
    outs.append(local(gin, o_gin))
    outs += gout_4()
    for cp in sent:
        cp.wait_send()
    for cp in outs:
        cp.wait()


def call(*args):
    vm = pltpu.VMEM
    out = [
        jax.ShapeDtypeStruct((ROWS, 1024), BF),
        jax.ShapeDtypeStruct((256, 256), F32),
        jax.ShapeDtypeStruct((8, 1024), F32),
        jax.ShapeDtypeStruct((1, 1024), F32),
        jax.ShapeDtypeStruct((1024, 256), F32),
        jax.ShapeDtypeStruct((32, 1024), F32),
        jax.ShapeDtypeStruct((1024, 256), F32),
        jax.ShapeDtypeStruct((32, 1024), F32),
        jax.ShapeDtypeStruct((1024, 256), F32),
        jax.ShapeDtypeStruct((32, 1024), F32),
    ]
    scratch = [
        vm((2, 2, 2, 4, 4, 128, 512), BF),
        vm((4, 4, 2, 2, 128, 256), BF),
        vm((ROWS, 8192), BF),
        vm((16, 8192), BF),
        vm((16, 8192), BF),
        vm((2, ROWS, 1024), BF),
        vm((4, 4, 2, 4, 64, 256), BF),
        vm((4, 2, 2, 2, 64, 256), BF),
        vm((4, 2, 4, 2, 64, 256), BF),
        vm((4, 2, 64, 256), BF),
        vm((4, 2, 2, 64, 256), BF),
        vm((4, 64, 256), BF),
        vm((ROWS, 1024), BF),
        vm((256, 1024), BF),
        vm((2, ROWS, 512), F32),
        vm((ROWS, 256), F32),
        vm((256, ROWS), BF),
        vm((ROWS, 1024), BF),
        vm((1, 8192), jnp.int32),
        vm((1, 1024), F32),
        vm((256, 512), BF),
        vm((2, 4, 4, 16, 512), BF),
        vm((2, 3, 4, 16, 512), BF),
        vm((2, 3, 16, 512), F32),
        vm((2, 8, 1024), F32),
        vm((2, 4, 16, 512), F32),
        vm((8, 1024), F32),
        vm((8, 1024), F32),
        vm((4, 1024, 256), F32),
        vm((4, 32, 1024), F32),
        vm((2, 512, 256), BF),
        vm((2, 16, 1024), BF),
        vm((512, 256), BF),
        vm((16, 1024), BF),
        vm((512, 256), BF),
        vm((16, 1024), BF),
        vm((256, 256), F32),
        vm((256, 256), F32),
        vm((2, 8, 1024), F32),
        pltpu.SemaphoreType.DMA((NSEM,)),
        pltpu.SemaphoreType.DMA((NSEM,)),
        pltpu.SemaphoreType.DMA((40,)),
        pltpu.SemaphoreType.DMA((2, 4)),
    ]
    hbm = pl.BlockSpec(memory_space=pl.ANY)
    return pl.pallas_call(
        body,
        name="step",
        out_shape=out,
        in_specs=[hbm] * len(args),
        out_specs=[hbm] * len(out),
        scratch_shapes=scratch,
        compiler_params=pltpu.CompilerParams(
            collective_id=0, has_side_effects=True, vmem_limit_bytes=64 * 1024 * 1024
        ),
        cost_estimate=pl.CostEstimate(flops=23_000_000_000, bytes_accessed=30_000_000, transcendentals=0),
    )(*args)


def hand_over(refs):
    n = len(refs)
    parts = []
    for k, a in enumerate(refs):
        parts.append((k, pl.ds(0, a.shape[0])))

    def copy_all(*args):
        src, dst, held = args[:n], args[n : 2 * n], args[2 * n : 3 * n]
        sem_in, sem_out = args[3 * n :]
        into, away = [], []
        for m, (k, rows) in enumerate(parts):
            into.append(pltpu.make_async_copy(src[k].at[rows], held[k].at[rows], sem_in.at[m]))
            away.append(pltpu.make_async_copy(held[k].at[rows], dst[k].at[rows], sem_out.at[m]))
        for cp in into:
            cp.start()
        for a, b in zip(into, away):
            a.wait()
            b.start()
        for cp in away:
            cp.wait()

    hbm = pl.BlockSpec(memory_space=pl.ANY)
    return pl.pallas_call(
        copy_all,
        name="hand_over",
        out_shape=[jax.ShapeDtypeStruct(a.shape, a.dtype) for a in refs],
        in_specs=[hbm] * n,
        out_specs=[hbm] * n,
        scratch_shapes=[pltpu.VMEM(a.shape, a.dtype) for a in refs]
        + [pltpu.SemaphoreType.DMA((len(parts),))] * 2,
        compiler_params=pltpu.CompilerParams(vmem_limit_bytes=60 * 1024 * 1024),
    )(*refs)


def per_device(
    tokens, sign_bits, base_weight, learned_column_scale, adapter_in, adapter_up_weight, out_cotangent,
    local_left, local_right, global_left, global_right, moment_left, moment_right, pending_left, pending_right,
):
    left = [a.reshape(1024, 256) for a in (local_left, global_left, moment_left, pending_left)]
    right = [a.reshape(32, 1024) for a in (local_right, global_right, moment_right, pending_right)]
    pairs = [a for pair in zip(left, right) for a in pair]
    out = call(
        tokens, sign_bits.reshape(1, 8192), base_weight, learned_column_scale.reshape(1, 1024),
        adapter_in.reshape(2, 128, 256), adapter_up_weight.reshape(256, 1024), out_cotangent, *pairs,
    )
    val, gin, gout, gs, gl, gr, ml, mr, pdl, pdr = out
    return hand_over((
        val, gin[None], gout[None], gs,
        gl.reshape(4, 256, 256), gr.reshape(4, 8, 1024), ml.reshape(4, 256, 256), mr.reshape(4, 8, 1024),
        pdl.reshape(4, 256, 256), pdr.reshape(4, 8, 1024),
    ))


def solution(mesh):
    rows, frag = P(("replica", "fsdp"), None), P(None, "fsdp", None)
    return jax.shard_map(
        per_device,
        mesh=mesh,
        in_specs=(
            rows, P(), P("fsdp", None), P(), P("replica", "fsdp", None), P("replica", None, None), rows,
            P("replica", None, "fsdp", None), P("replica", None, "fsdp", None),
        ) + (frag,) * 6,
        out_specs=(rows, P("replica", "fsdp", None), P("replica", "fsdp", None), P("replica", None)) + (frag,) * 6,
        check_vma=False,
    )
```
